256 devices in a mesh: layer: 4 (over z_lo, core), latent: 64 (over x, y, z_hi).
Axes of the slice: x: 4, y: 4, z: 8 (z_hi: 4, z_lo: 2; z = z_hi * 2 + z_lo), core: 2. Of those that a mesh axis runs over, the one named last changes fastest.
Arguments:
- streams: bfloat16 [4, 1024, 4096], P('layer', 'latent'), may hold values from -6 to 6
- enc_weight: bfloat16 [4, 4096, 32768], P('layer', None, 'latent'), may hold values from -0.046875 to 0.046875
- enc_bias: float32 [32768], P('latent'), may hold values from -3 to 3
- dec_weight: bfloat16 [4, 32768, 4096], P('layer', 'latent'), may hold values from -0.046875 to 0.046875
- dec_bias: float32 [4, 4096], P('layer'), may hold values from -3 to 3
Outputs:
- recon: float32 [4, 1024, 4096], P('layer', 'latent')
The draws below stay inside these ranges and needn't reach their ends.
All inputs are finite; a program needn't handle non-finite values.
Results may differ from the reference program's by a relative error of at most 0.0027.
Values may be sent and summed in bfloat16 or wider, within the bound.
A program may use at most 128 MiB of HBM per device.

```python
import jax
import jax.numpy as jnp

D = 4096
TOKENS = 1024
LAYERS = 4
LATENTS = 32768


def block_scale(stream_key, shape, shards, low, top_value):
    factor_of, own = 1.0, jax.random.fold_in(stream_key, 6)
    for axis_at, parts in shards:
        heights = jnp.exp(jax.random.uniform(jax.random.fold_in(own, axis_at), (parts,), jnp.float32, low / len(shards), top_value / len(shards)))
        factor_of = factor_of * jnp.repeat(heights, shape[axis_at] // parts).reshape([-1 if axis == axis_at else 1 for axis in range(len(shape))])
    return factor_of


def noise(rng, shape, spread, most, pieces=(), kind=jnp.bfloat16):
    factor_of = block_scale(rng, shape, pieces, -0.22, 0.18) if pieces else 1.0
    result = jax.random.normal(rng, shape, jnp.float32) * spread * factor_of
    return jnp.minimum(jnp.maximum(result, -most), most).astype(kind)


def setup_inputs(seed: int = 0) -> dict:
    streams_of = jax.random.split(jax.random.key(seed), 6)
    return {
        "streams": noise(streams_of[0], (LAYERS, TOKENS, D), 1.0, 6.0, ((0, 4), (1, 64))),
        "enc_weight": noise(streams_of[1], (LAYERS, D, LATENTS), (D * LAYERS) ** -0.5, 0.046875, ((0, 4), (2, 64))),
        "enc_bias": noise(streams_of[2], (LATENTS,), 0.5, 3.0, ((0, 64),), jnp.float32),
        "dec_weight": noise(streams_of[3], (LAYERS, LATENTS, D), (LATENTS // 2) ** -0.5, 0.046875, ((0, 4), (1, 64))),
        "dec_bias": noise(streams_of[4], (LAYERS, D), 0.5, 3.0, ((0, 4),), jnp.float32),
    }


def reference(streams, enc_weight, enc_bias, dec_weight, dec_bias):
    pre = jnp.zeros((streams.shape[1], enc_weight.shape[2]), jnp.float32)
    for layer_idx in range(LAYERS):
        pre = pre + jnp.dot(streams[layer_idx], enc_weight[layer_idx], preferred_element_type=jnp.float32)
    pre = pre + enc_bias[None, :]
    codes = jnp.maximum(pre, 0.0).astype(jnp.bfloat16)
    outputs = []
    for layer_idx in range(LAYERS):
        term = jnp.dot(codes, dec_weight[layer_idx], preferred_element_type=jnp.float32)
        outputs.append(term + dec_bias[layer_idx][None, :])
    return jnp.stack(outputs, axis=0)
```

```python
import functools

import jax
import jax.numpy as jnp
from jax import lax
from jax.experimental import pallas as pl
from jax.experimental.pallas import tpu as pltpu
from jax.sharding import PartitionSpec as P

MESH = pl.DeviceIdType.MESH
F32, BF16 = jnp.float32, jnp.bfloat16
OFF = (0, 1, 3, 2)
NK = 4
ROWS, D, M, HALF = 16, 4096, 512, 2048
A_STEPS = (1, 3, 2)

PROGRAM = (
    "A0", "Z", "B02", "B00", "C00", "B01", "C01", "C02", "A1", "C03", "A2", "A3",
    "B10", "B12", "B11", "D0", "B21", "B20", "B22", "C13", "C10", "X0", "C11", "C12",
    "C23", "C22", "C21", "C20", "B30", "B32", "Y0", "D1", "X1", "B31", "E00", "E01",
    "D2", "X2", "C31", "C33", "C32", "C30", "Y1", "E10", "E11", "D3", "F011", "F010",
    "Y2", "F000", "F001", "F100", "F111", "F101", "F110", "X3", "G01", "G00", "G11", "G10",
    "H00", "E20", "H01", "E21", "Y3", "H11", "H10", "E30", "E31", "F200", "F201", "F210",
    "F211", "F301", "F300", "G20", "G21", "F310", "F311", "H20", "G30", "H21", "G31", "H30",
    "H31",
)


def kernel(
    s_ref, we_hbm, eb_ref, wd_hbm, out_ref,
    g, we, wd, part, cx, q, zx, codes, full, ob, r1, r2, asnd, arcv, zsnd, zrcv, acc,
    lsem, ag_s, ag_r, zg_s, zg_r, x_s, x_r, rs_s, rs_r,
):
    lay, lat = lax.axis_index("layer"), lax.axis_index("latent")
    zlo, core = lay // 2, lay % 2
    x, y, z = lat // 16, (lat // 4) % 4, lat % 4
    m4 = lambda v: lax.rem(v + 8, 4)

    def dev(dx=0, dy=0, dz=0, dl=0, dc=0):
        return (
            lax.rem(zlo + dl, 2) * 2 + lax.rem(core + dc, 2),
            (m4(x + dx) * 4 + m4(y + dy)) * 4 + m4(z + dz),
        )

    def a_dev(h, d):
        return dev(dy=d) if h == 0 else dev(dx=d)

    def b_dev(h, d):
        return dev(dx=d) if h == 0 else dev(dy=d)

    ca = (y, x)
    cb = (x, y)
    cols = tuple(pl.ds(h * HALF, HALF) for h in range(2))

    def slot(buf, k, h, b, a):
        return buf.at[k, b, a, :, cols[h]] if h == 0 else buf.at[k, a, b, :, cols[h]]

    def span(buf, k, h, b, a0, n):
        return buf.at[k, b, pl.ds(a0, n), :, cols[h]] if h == 0 else buf.at[k, pl.ds(a0, n), b, :, cols[h]]

    def push(src, dst, ssem, rsem, target):
        return pltpu.make_async_remote_copy(
            src_ref=src, dst_ref=dst, send_sem=ssem, recv_sem=rsem, device_id=target, device_id_type=MESH
        )

    sent = []

    def start(copy):
        copy.start()
        sent.append(copy)

    load_s = pltpu.make_async_copy(s_ref.at[0], g.at[0, x, y], lsem.at[0])
    load_e = pltpu.make_async_copy(we_hbm.at[0], we, lsem.at[1])
    load_d = pltpu.make_async_copy(wd_hbm.at[0], wd, lsem.at[2])
    load_s.start()
    load_e.start()
    load_d.start()
    bar = pltpu.get_barrier_semaphore()
    partners = [dev(dx=d) for d in (1, 2, 3)] + [dev(dy=d) for d in (1, 2, 3)]
    partners += [dev(dz=d) for d in (1, 2, 3)] + [dev(dc=1), dev(dl=1)]
    for p in partners:
        pl.semaphore_signal(bar, inc=1, device_id=p, device_id_type=MESH)
    pl.semaphore_wait(bar, len(partners))
    load_s.wait()

    def zg(k):
        return push(g.at[0, x, y], g.at[k, x, y], zg_s.at[k], zg_r.at[k], dev(dz=4 - OFF[k]))

    def ag(k, h, i):
        a, b = ca[h], cb[h]
        if i < 3:
            src, target = slot(g, k, h, b, a), a_dev(h, A_STEPS[i])
        elif i < 11:
            j, way = (i - 3) // 2, (i - 3) % 2
            src, target = slot(g, k, h, b, m4(a + j)), b_dev(h, 1 if way == 0 else 3)
        else:
            j = i - 11
            src = slot(g, k, h, m4(b + (3 if j % 2 == 0 else 1)), m4(a + j))
            target = b_dev(h, 1 if j % 2 == 0 else 3)
        return push(src, src, ag_s.at[k, h, i], ag_r.at[k, h, i], target)

    def step_z():
        for i in range(1, NK):
            start(zg(i))

    def step_a(k):
        if k:
            zg(k).wait_recv()
        for h in range(2):
            for i in (0, 1, 3, 4, 2):
                start(ag(k, h, i))

    def step_b(k, i):
        j = (4 - A_STEPS[i]) % 4
        for h in range(2):
            ag(k, h, i).wait_recv()
            start(ag(k, h, 3 + 2 * j))
            start(ag(k, h, 4 + 2 * j))

    def step_c(k, j):
        for h in range(2):
            ag(k, h, 3 + 2 * j + j % 2).wait_recv()
            start(ag(k, h, 11 + j))

    def step_w(k):
        for h in range(2):
            for j in range(4):
                ag(k, h, 3 + 2 * j + 1 - j % 2).wait_recv()
        for h in range(2):
            for j in range(4):
                ag(k, h, 11 + j).wait_recv()

    def xch(k, i):
        if i == 0:
            return push(part.at[k, 1 - core], cx.at[k], x_s.at[k, 0], x_r.at[k, 0], dev(dc=1))
        if i == 1:
            return push(q.at[k], zx.at[k], x_s.at[k, 1], x_r.at[k, 1], dev(dl=1))
        mine = codes.at[k, pl.ds(2 * core, 2)]
        return push(mine, mine, x_s.at[k, 2], x_r.at[k, 2], dev(dc=1))

    loaded = []

    def step_d(k):
        step_w(k)
        if not loaded:
            load_e.wait()
            load_d.wait()
            loaded.append(k)
        rows = g.at[k]

        def body(n, c):
            at = pl.ds(pl.multiple_of(n * 256, 256), 256)
            lhs = rows[...].reshape(256, D)
            r = jnp.dot(lhs, we[:, at], preferred_element_type=F32)
            part[k, :, :, at] = r.reshape(2, 128, 256)
            return c

        lax.fori_loop(0, 2, body, 0)
        start(xch(k, 0))

    def step_x(k):
        xch(k, 0).wait_recv()
        q[k] = part[k, core] + cx[k]
        start(xch(k, 1))

    def step_y(k):
        xch(k, 1).wait_recv()
        pre = q[k] + zx[k] + eb_ref[...]
        codes[k, pl.ds(2 * core, 2)] = jnp.maximum(pre, 0.0).astype(BF16).reshape(2, 4, ROWS, M)
        start(xch(k, 2))

    def rs(k, h, i):
        a, b = ca[h], cb[h]
        if i == 0:
            src, dst, t = span(ob, k, h, m4(b + 2), 0, 2), r1.at[k, h, 0], b_dev(h, 1)
        elif i == 1:
            src, dst, t = span(ob, k, h, m4(b + 2), 2, 2), r1.at[k, h, 1], b_dev(h, 3)
        elif i == 2:
            src, dst, t = span(ob, k, h, m4(b + 1), 2, 2), r2.at[k, h, 0, pl.ds(2, 2)], b_dev(h, 1)
        elif i == 3:
            src, dst, t = span(ob, k, h, m4(b + 3), 0, 2), r2.at[k, h, 1, pl.ds(0, 2)], b_dev(h, 3)
        elif i == 4:
            src, dst, t = span(ob, k, h, m4(b + 1), 0, 2), r2.at[k, h, 0, pl.ds(0, 2)], b_dev(h, 1)
        elif i == 5:
            src, dst, t = span(ob, k, h, m4(b + 3), 2, 2), r2.at[k, h, 1, pl.ds(2, 2)], b_dev(h, 3)
        elif i < 9:
            d = A_STEPS[i - 6]
            src, dst, t = asnd.at[k, h, m4(a + d)], arcv.at[k, h, i - 6], a_dev(h, d)
        else:
            src, dst, t = zsnd.at[k, :, cols[h]], zrcv.at[k, :, cols[h]], dev(dz=OFF[k])
        return push(src, dst, rs_s.at[k, h, i], rs_r.at[k, h, i], t)

    def step_e(k, h):
        if h == 0:
            xch(k, 2).wait_recv()

        def body(n, c):
            at = pl.ds(pl.multiple_of(h * HALF + n * 512, 512), 512)
            r = jnp.dot(codes[k].reshape(256, M), wd[:, at], preferred_element_type=F32)
            r = r.reshape(4, 4, ROWS, 512)
            full[k % 2, :, :, :, at] = r
            ob[k, :, :, :, at] = r.astype(BF16)
            return c

        lax.fori_loop(0, HALF // 512, body, 0)
        for i in range(4):
            start(rs(k, h, i))

    def tiles(width, step, body):
        def run(n, c):
            body(pl.multiple_of(n * step, step))
            return c

        lax.fori_loop(0, width // step, run, 0)

    def step_f(k, h, w):
        rs(k, h, w).wait_recv()
        to = m4(cb[h] + (1 if w == 0 else 3))
        rows = pl.ds(0 if w == 0 else 2, 2)

        def body(c0):
            at = pl.ds(h * HALF + c0, 512)
            got = r1[k, h, w, :, :, pl.ds(c0, 512)].astype(F32)
            if h == 0:
                ob[k, to, rows, :, at] = (full[k % 2, to, rows, :, at] + got).astype(BF16)
            else:
                ob[k, rows, to, :, at] = (full[k % 2, rows, to, :, at] + got).astype(BF16)

        tiles(HALF, 512, body)
        start(rs(k, h, 4 + w))

    def step_g(k, h):
        for i in (2, 3, 4, 5):
            rs(k, h, i).wait_recv()
        b = cb[h]

        def body(c0):
            at = pl.ds(h * HALF + c0, 512)
            got = r2[k, h, 0, :, :, pl.ds(c0, 512)].astype(F32) + r2[k, h, 1, :, :, pl.ds(c0, 512)].astype(F32)
            if h == 0:
                s = full[k % 2, b, :, :, at] + got
                full[k % 2, b, :, :, at] = s
            else:
                s = full[k % 2, :, b, :, at] + got
                full[k % 2, :, b, :, at] = s
            asnd[k, h, :, :, pl.ds(c0, 512)] = s.astype(BF16)

        tiles(HALF, 512, body)
        for i in (6, 7, 8):
            start(rs(k, h, i))

    def step_h(k, h):
        for i in (6, 7, 8):
            rs(k, h, i).wait_recv()
        at = cols[h]
        s = full[k % 2, x, y, :, at]
        for i in range(3):
            s = s + arcv[k, h, i].astype(F32)
        if k == 0:
            acc[:, at] = s
        else:
            zsnd[k, :, at] = s.astype(BF16)
            start(rs(k, h, 9))

    steps = dict(
        Z=step_z, A=step_a, B=step_b, C=step_c, D=step_d, X=step_x, Y=step_y, E=step_e, F=step_f, G=step_g, H=step_h
    )
    for name in PROGRAM:
        steps[name[0]](*(int(v) for v in name[1:]))

    for k in range(1, NK):
        for h in range(2):
            rs(k, h, 9).wait_recv()
    total = acc[...]
    for k in range(1, NK):
        total = total + zrcv[k].astype(F32)
    out_ref[...] = total
    for copy in sent:
        copy.wait_send()


def shards(streams, enc_weight, enc_bias, dec_weight, dec_bias):
    dma = pltpu.SemaphoreType.DMA
    any_space, vmem = pl.BlockSpec(memory_space=pl.ANY), pl.BlockSpec(memory_space=pltpu.VMEM)
    rows = pl.pallas_call(
        kernel,
        out_shape=jax.ShapeDtypeStruct((ROWS, D), F32),
        in_specs=[any_space, any_space, vmem, any_space],
        out_specs=vmem,
        scratch_shapes=[
            pltpu.VMEM((NK, 4, 4, ROWS, D), BF16),
            pltpu.VMEM((D, M), BF16),
            pltpu.VMEM((M, D), BF16),
            pltpu.VMEM((NK, 2, 128, M), F32),
            pltpu.VMEM((NK, 128, M), F32),
            pltpu.VMEM((NK, 128, M), F32),
            pltpu.VMEM((NK, 128, M), F32),
            pltpu.VMEM((NK, 4, 4, ROWS, M), BF16),
            pltpu.VMEM((2, 4, 4, ROWS, D), F32),
            pltpu.VMEM((NK, 4, 4, ROWS, D), BF16),
            pltpu.VMEM((NK, 2, 2, 2, ROWS, HALF), BF16),
            pltpu.VMEM((NK, 2, 2, 4, ROWS, HALF), BF16),
            pltpu.VMEM((NK, 2, 4, ROWS, HALF), BF16),
            pltpu.VMEM((NK, 2, 3, ROWS, HALF), BF16),
            pltpu.VMEM((NK, ROWS, D), BF16),
            pltpu.VMEM((NK, ROWS, D), BF16),
            pltpu.VMEM((ROWS, D), F32),
            dma((3,)),
            dma((NK, 2, 15)),
            dma((NK, 2, 15)),
            dma((NK,)),
            dma((NK,)),
            dma((NK, 3)),
            dma((NK, 3)),
            dma((NK, 2, 10)),
            dma((NK, 2, 10)),
        ],
        compiler_params=pltpu.CompilerParams(
            collective_id=1, has_side_effects=True, vmem_limit_bytes=60 * 1024 * 1024
        ),
        cost_estimate=pl.CostEstimate(flops=8 * 1024 * D * M, bytes_accessed=9 * 1024 * 1024, transcendentals=0),
        name="crosscoder",
    )(streams, enc_weight, enc_bias.reshape(1, M), dec_weight)
    return (rows + dec_bias)[None]


def solution(mesh):
    in_specs = (
        P("layer", "latent", None),
        P("layer", None, "latent"),
        P("latent"),
        P("layer", "latent", None),
        P("layer", None),
    )
    return jax.shard_map(
        shards, mesh=mesh, in_specs=in_specs, out_specs=P("layer", "latent", None), check_vma=False
    )
```

```python
import functools

import jax
import jax.numpy as jnp
from jax import lax
from jax.experimental import pallas as pl
from jax.experimental.pallas import tpu as pltpu
from jax.sharding import PartitionSpec as P

MESH = pl.DeviceIdType.MESH
F32, BF16 = jnp.float32, jnp.bfloat16
OFF = (0, 1, 3, 2)
NK = 4
ROWS, D, M, HALF = 16, 4096, 512, 2048
A_STEPS = (1, 3, 2)

PROGRAM = (
    "Z2", "A0", "Z1", "B00", "B01", "A1", "B02", "A2", "C00", "B10", "Z3", "B11",
    "C03", "C01", "C02", "B12", "A3", "B20", "C11", "C13", "C12", "C10", "D0", "X0",
    "B31", "B30", "B21", "B32", "D1", "C33", "C31", "B22", "Y0", "X1", "C30", "C32",
    "C21", "C22", "C20", "C23", "E00", "E01", "D3", "Y1", "X3", "E10", "E11", "D2",
    "X2", "F010", "F000", "F011", "Y3", "F001", "E30", "E31", "Y2", "E20", "E21", "F101",
    "F100", "F300", "F310", "F301", "F311", "F111", "F110", "F201", "F200", "F211", "F210", "G31",
    "G30", "G20", "G11", "H31", "G10", "H30", "G21", "H20", "H11", "H21", "H10", "G01",
    "G00", "H01", "H00",
)


def kernel(
    s_ref, we_hbm, eb_ref, wd_hbm, out_ref,
    g, we, wd, part, cx, q, zx, codes, full, ob, r1, r2, asnd, arcv, zsnd, zrcv, acc,
    lsem, ag_s, ag_r, zg_s, zg_r, x_s, x_r, rs_s, rs_r,
):
    lay, lat = lax.axis_index("layer"), lax.axis_index("latent")
    zlo, core = lay // 2, lay % 2
    x, y, z = lat // 16, (lat // 4) % 4, lat % 4
    m4 = lambda v: lax.rem(v + 8, 4)

    def dev(dx=0, dy=0, dz=0, dl=0, dc=0):
        return (
            lax.rem(zlo + dl, 2) * 2 + lax.rem(core + dc, 2),
            (m4(x + dx) * 4 + m4(y + dy)) * 4 + m4(z + dz),
        )

    def a_dev(h, d):
        return dev(dy=d) if h == 0 else dev(dx=d)

    def b_dev(h, d):
        return dev(dx=d) if h == 0 else dev(dy=d)

    ca = (y, x)
    cb = (x, y)
    cols = tuple(pl.ds(h * HALF, HALF) for h in range(2))

    def slot(buf, k, h, b, a):
        return buf.at[k, b, a, :, cols[h]] if h == 0 else buf.at[k, a, b, :, cols[h]]

    def span(buf, k, h, b, a0, n):
        return buf.at[k, b, pl.ds(a0, n), :, cols[h]] if h == 0 else buf.at[k, pl.ds(a0, n), b, :, cols[h]]

    def push(src, dst, ssem, rsem, target):
        return pltpu.make_async_remote_copy(
            src_ref=src, dst_ref=dst, send_sem=ssem, recv_sem=rsem, device_id=target, device_id_type=MESH
        )

    sent = []

    def start(copy):
        copy.start()
        sent.append(copy)

    load_s = pltpu.make_async_copy(s_ref.at[0], g.at[0, x, y], lsem.at[0])
    load_e = pltpu.make_async_copy(we_hbm.at[0], we, lsem.at[1])
    load_d = pltpu.make_async_copy(wd_hbm.at[0], wd, lsem.at[2])
    load_s.start()
    load_e.start()
    load_d.start()
    bar = pltpu.get_barrier_semaphore()
    partners = [dev(dx=d) for d in (1, 2, 3)] + [dev(dy=d) for d in (1, 2, 3)]
    partners += [dev(dz=d) for d in (1, 2, 3)] + [dev(dc=1), dev(dl=1)]
    for p in partners:
        pl.semaphore_signal(bar, inc=1, device_id=p, device_id_type=MESH)
    pl.semaphore_wait(bar, len(partners))
    load_s.wait()

    def zg(k):
        return push(g.at[0, x, y], g.at[k, x, y], zg_s.at[k], zg_r.at[k], dev(dz=4 - OFF[k]))

    def ag(k, h, i):
        a, b = ca[h], cb[h]
        if i < 2:
            src, target = slot(g, k, h, b, a), a_dev(h, A_STEPS[i])
        elif i == 2 or i == 15:
            from_a, w = (m4(a + 3), 0) if i == 2 else (m4(a + 1), 1)
            at = pl.ds(h * HALF + w * (HALF // 2), HALF // 2)
            src = g.at[k, b, from_a, :, at] if h == 0 else g.at[k, from_a, b, :, at]
            target = a_dev(h, 1 if i == 2 else 3)
        elif i < 11:
            j, way = (i - 3) // 2, (i - 3) % 2
            src, target = slot(g, k, h, b, m4(a + j)), b_dev(h, 1 if way == 0 else 3)
        else:
            j = i - 11
            src = slot(g, k, h, m4(b + (3 if j % 2 == 0 else 1)), m4(a + j))
            target = b_dev(h, 1 if j % 2 == 0 else 3)
        return push(src, src, ag_s.at[k, h, i], ag_r.at[k, h, i], target)

    def step_z(k):
        start(zg(k))

    def step_a(k):
        if k:
            zg(k).wait_recv()
        for h in range(2):
            for i in (0, 1, 3, 4):
                start(ag(k, h, i))

    def step_b(k, i):
        j = (4 - A_STEPS[i]) % 4
        for h in range(2):
            ag(k, h, i).wait_recv()
            if i == 2:
                ag(k, h, 15).wait_recv()
            else:
                start(ag(k, h, 2 if i == 0 else 15))
            start(ag(k, h, 3 + 2 * j))
            start(ag(k, h, 4 + 2 * j))

    def step_c(k, j):
        for h in range(2):
            ag(k, h, 3 + 2 * j + j % 2).wait_recv()
            start(ag(k, h, 11 + j))

    def step_w(k):
        for h in range(2):
            for j in range(4):
                ag(k, h, 3 + 2 * j + 1 - j % 2).wait_recv()
        for h in range(2):
            for j in range(4):
                ag(k, h, 11 + j).wait_recv()

    def xch(k, i):
        if i == 0:
            return push(part.at[k, 1 - core], cx.at[k], x_s.at[k, 0], x_r.at[k, 0], dev(dc=1))
        if i == 1:
            return push(q.at[k], zx.at[k], x_s.at[k, 1], x_r.at[k, 1], dev(dl=1))
        mine = codes.at[k, pl.ds(2 * core, 2)]
        return push(mine, mine, x_s.at[k, 2], x_r.at[k, 2], dev(dc=1))

    loaded = []

    def step_d(k):
        step_w(k)
        if not loaded:
            load_e.wait()
            load_d.wait()
            loaded.append(k)
        rows = g.at[k]

        def body(n, c):
            at = pl.ds(pl.multiple_of(n * 256, 256), 256)
            lhs = rows[...].reshape(256, D)
            r = jnp.dot(lhs, we[:, at], preferred_element_type=F32)
            part[k, :, :, at] = r.reshape(2, 128, 256)
            return c

        lax.fori_loop(0, 2, body, 0)
        start(xch(k, 0))

    def step_x(k):
        xch(k, 0).wait_recv()
        q[k] = part[k, core] + cx[k]
        start(xch(k, 1))

    def step_y(k):
        xch(k, 1).wait_recv()
        pre = q[k] + zx[k] + eb_ref[...]
        codes[k, pl.ds(2 * core, 2)] = jnp.maximum(pre, 0.0).astype(BF16).reshape(2, 4, ROWS, M)
        start(xch(k, 2))

    def rs(k, h, i):
        a, b = ca[h], cb[h]
        if i == 0:
            src, dst, t = span(ob, k, h, m4(b + 2), 0, 2), r1.at[k, h, 0], b_dev(h, 1)
        elif i == 1:
            src, dst, t = span(ob, k, h, m4(b + 2), 2, 2), r1.at[k, h, 1], b_dev(h, 3)
        elif i == 2:
            src, dst, t = span(ob, k, h, m4(b + 1), 2, 2), r2.at[k, h, 0, pl.ds(2, 2)], b_dev(h, 1)
        elif i == 3:
            src, dst, t = span(ob, k, h, m4(b + 3), 0, 2), r2.at[k, h, 1, pl.ds(0, 2)], b_dev(h, 3)
        elif i == 4:
            src, dst, t = span(ob, k, h, m4(b + 1), 0, 2), r2.at[k, h, 0, pl.ds(0, 2)], b_dev(h, 1)
        elif i == 5:
            src, dst, t = span(ob, k, h, m4(b + 3), 2, 2), r2.at[k, h, 1, pl.ds(2, 2)], b_dev(h, 3)
        elif i < 9:
            d = A_STEPS[i - 6]
            src, dst, t = asnd.at[k, h, m4(a + d)], arcv.at[k, h, i - 6], a_dev(h, d)
        else:
            src, dst, t = zsnd.at[k, :, cols[h]], zrcv.at[k, :, cols[h]], dev(dz=OFF[k])
        return push(src, dst, rs_s.at[k, h, i], rs_r.at[k, h, i], t)

    def step_e(k, h):
        if h == 0:
            xch(k, 2).wait_recv()

        def body(n, c):
            at = pl.ds(pl.multiple_of(h * HALF + n * 512, 512), 512)
            r = jnp.dot(codes[k].reshape(256, M), wd[:, at], preferred_element_type=F32)
            r = r.reshape(4, 4, ROWS, 512)
            full[k, :, :, :, at] = r
            ob[k, :, :, :, at] = r.astype(BF16)
            return c

        lax.fori_loop(0, HALF // 512, body, 0)
        for i in range(4):
            start(rs(k, h, i))

    def tiles(width, step, body):
        def run(n, c):
            body(pl.multiple_of(n * step, step))
            return c

        lax.fori_loop(0, width // step, run, 0)

    def step_f(k, h, w):
        rs(k, h, w).wait_recv()
        to = m4(cb[h] + (1 if w == 0 else 3))
        rows = pl.ds(0 if w == 0 else 2, 2)

        def body(c0):
            at = pl.ds(h * HALF + c0, 512)
            got = r1[k, h, w, :, :, pl.ds(c0, 512)].astype(F32)
            if h == 0:
                ob[k, to, rows, :, at] = (full[k, to, rows, :, at] + got).astype(BF16)
            else:
                ob[k, rows, to, :, at] = (full[k, rows, to, :, at] + got).astype(BF16)

        tiles(HALF, 512, body)
        start(rs(k, h, 4 + w))

    def step_g(k, h):
        for i in (2, 3, 4, 5):
            rs(k, h, i).wait_recv()
        b = cb[h]

        def body(c0):
            at = pl.ds(h * HALF + c0, 512)
            got = r2[k, h, 0, :, :, pl.ds(c0, 512)].astype(F32) + r2[k, h, 1, :, :, pl.ds(c0, 512)].astype(F32)
            if h == 0:
                s = full[k, b, :, :, at] + got
                full[k, b, :, :, at] = s
            else:
                s = full[k, :, b, :, at] + got
                full[k, :, b, :, at] = s
            asnd[k, h, :, :, pl.ds(c0, 512)] = s.astype(BF16)

        tiles(HALF, 512, body)
        for i in (6, 7, 8):
            start(rs(k, h, i))

    def step_h(k, h):
        for i in (6, 7, 8):
            rs(k, h, i).wait_recv()
        at = cols[h]
        s = full[k, x, y, :, at]
        for i in range(3):
            s = s + arcv[k, h, i].astype(F32)
        if k == 0:
            acc[:, at] = s
        else:
            zsnd[k, :, at] = s.astype(BF16)
            start(rs(k, h, 9))

    steps = dict(
        Z=step_z, A=step_a, B=step_b, C=step_c, D=step_d, X=step_x, Y=step_y, E=step_e, F=step_f, G=step_g, H=step_h
    )
    for name in PROGRAM:
        steps[name[0]](*(int(v) for v in name[1:]))

    for k in range(1, NK):
        for h in range(2):
            rs(k, h, 9).wait_recv()
    total = acc[...]
    for k in range(1, NK):
        total = total + zrcv[k].astype(F32)
    out_ref[...] = total
    for copy in sent:
        copy.wait_send()


def shards(streams, enc_weight, enc_bias, dec_weight, dec_bias):
    dma = pltpu.SemaphoreType.DMA
    any_space, vmem = pl.BlockSpec(memory_space=pl.ANY), pl.BlockSpec(memory_space=pltpu.VMEM)
    rows = pl.pallas_call(
        kernel,
        out_shape=jax.ShapeDtypeStruct((ROWS, D), F32),
        in_specs=[any_space, any_space, vmem, any_space],
        out_specs=vmem,
        scratch_shapes=[
            pltpu.VMEM((NK, 4, 4, ROWS, D), BF16),
            pltpu.VMEM((D, M), BF16),
            pltpu.VMEM((M, D), BF16),
            pltpu.VMEM((NK, 2, 128, M), F32),
            pltpu.VMEM((NK, 128, M), F32),
            pltpu.VMEM((NK, 128, M), F32),
            pltpu.VMEM((NK, 128, M), F32),
            pltpu.VMEM((NK, 4, 4, ROWS, M), BF16),
            pltpu.VMEM((4, 4, 4, ROWS, D), F32),
            pltpu.VMEM((NK, 4, 4, ROWS, D), BF16),
            pltpu.VMEM((NK, 2, 2, 2, ROWS, HALF), BF16),
            pltpu.VMEM((NK, 2, 2, 4, ROWS, HALF), BF16),
            pltpu.VMEM((NK, 2, 4, ROWS, HALF), BF16),
            pltpu.VMEM((NK, 2, 3, ROWS, HALF), BF16),
            pltpu.VMEM((NK, ROWS, D), BF16),
            pltpu.VMEM((NK, ROWS, D), BF16),
            pltpu.VMEM((ROWS, D), F32),
            dma((3,)),
            dma((NK, 2, 16)),
            dma((NK, 2, 16)),
            dma((NK,)),
            dma((NK,)),
            dma((NK, 3)),
            dma((NK, 3)),
            dma((NK, 2, 10)),
            dma((NK, 2, 10)),
        ],
        compiler_params=pltpu.CompilerParams(
            collective_id=1, has_side_effects=True, vmem_limit_bytes=61 * 1024 * 1024
        ),
        cost_estimate=pl.CostEstimate(flops=8 * 1024 * D * M, bytes_accessed=9 * 1024 * 1024, transcendentals=0),
        name="crosscoder",
    )(streams, enc_weight, enc_bias.reshape(1, M), dec_weight)
    return (rows + dec_bias)[None]


def solution(mesh):
    in_specs = (
        P("layer", "latent", None),
        P("layer", None, "latent"),
        P("latent"),
        P("layer", "latent", None),
        P("layer", None),
    )
    return jax.shard_map(
        shards, mesh=mesh, in_specs=in_specs, out_specs=P("layer", "latent", None), check_vma=False
    )
```

```python
import functools

import jax
import jax.numpy as jnp
from jax import lax
from jax.experimental import pallas as pl
from jax.experimental.pallas import tpu as pltpu
from jax.sharding import PartitionSpec as P

MESH = pl.DeviceIdType.MESH
F32, BF16 = jnp.float32, jnp.bfloat16
OFF = (0, 1, 3, 2)
NK = 4
ROWS, D, M, HALF = 16, 4096, 512, 2048
A_STEPS = (1, 3, 2)
EDGE = 256
SIDE = (D - EDGE) // 2
WHOLE = ()

PROGRAM = (
    "Z1", "Z2", "A0", "C00", "B01", "A1", "A2", "B11", "B10", "B21", "B12", "C10",
    "Z3", "C13", "C11", "B20", "C12", "B22", "A3", "C22", "C21", "C23", "C20", "D1",
    "B31", "X1", "B30", "B00", "D2", "X2", "C01", "B32", "B02", "Y1", "C31", "C33",
    "C30", "C32", "U1", "E10", "E11", "Y2", "C02", "D3", "C03", "U2", "E20", "X3",
    "E21", "D0", "F100", "F101", "F111", "F110", "F200", "Y3", "F201", "X0", "F210", "F211",
    "U3", "E30", "E31", "G21", "G11", "G10", "F300", "G20", "Y0", "F301", "F311", "F310",
    "E00", "E01", "H21", "H20", "G31", "G30", "H11", "H10", "F000", "F001", "F010", "F011",
    "H31", "H30", "G00", "G01", "H00", "H01",
)


def kernel(
    s_ref, we_hbm, eb_ref, wd_hbm, out_ref,
    g, we, wd, part, cx, q, zx, codes, full, ob, r1, r2, asnd, arcv, zsnd, zrcv, usnd, urcv, acc,
    lsem, ag_s, ag_r, zg_s, zg_r, x_s, x_r, rs_s, rs_r, u_s, u_r,
):
    lay, lat = lax.axis_index("layer"), lax.axis_index("latent")
    zlo, core = lay // 2, lay % 2
    x, y, z = lat // 16, (lat // 4) % 4, lat % 4
    m4 = lambda v: lax.rem(v + 8, 4)

    def dev(dx=0, dy=0, dz=0, dl=0, dc=0):
        return (
            lax.rem(zlo + dl, 2) * 2 + lax.rem(core + dc, 2),
            (m4(x + dx) * 4 + m4(y + dy)) * 4 + m4(z + dz),
        )

    def a_dev(h, d):
        return dev(dy=d) if h == 0 else dev(dx=d)

    def b_dev(h, d):
        return dev(dx=d) if h == 0 else dev(dy=d)

    ca = (y, x)
    cb = (x, y)
    cols = tuple(pl.ds(h * HALF, HALF) for h in range(2))

    def push(src, dst, ssem, rsem, target):
        return pltpu.make_async_remote_copy(
            src_ref=src, dst_ref=dst, send_sem=ssem, recv_sem=rsem, device_id=target, device_id_type=MESH
        )

    sent = []

    def start(copy):
        copy.start()
        sent.append(copy)

    load_s = [pltpu.make_async_copy(s_ref.at[0, :, cols[h]], g.at[0, h, cb[h], ca[h]], lsem.at[2 + h]) for h in range(2)]
    load_e = pltpu.make_async_copy(we_hbm.at[0], we, lsem.at[1])
    load_d = pltpu.make_async_copy(wd_hbm.at[0], wd, lsem.at[0])
    for copy in load_s:
        copy.start()
    load_e.start()
    load_d.start()
    bar = pltpu.get_barrier_semaphore()
    partners = [dev(dx=d) for d in (1, 2, 3)] + [dev(dy=d) for d in (1, 2, 3)]
    partners += [dev(dz=d) for d in (1, 2, 3)] + [dev(dc=1), dev(dl=1)]
    for p in partners:
        pl.semaphore_signal(bar, inc=1, device_id=p, device_id_type=MESH)
    pl.semaphore_wait(bar, len(partners))
    for copy in load_s:
        copy.wait()

    def zg(k, h):
        at = (h, cb[h], ca[h])
        return push(g.at[(0, *at)], g.at[(k, *at)], zg_s.at[k, h], zg_r.at[k, h], dev(dz=4 - OFF[k]))

    def ag(k, h, i):
        a, b = ca[h], cb[h]
        if i < 2:
            src, target = g.at[k, h, b, a], a_dev(h, A_STEPS[i])
        elif i == 2:
            src, target = g.at[k, h, b, m4(a + 3), :, pl.ds(0, HALF // 2)], a_dev(h, 1)
        elif i == 15:
            src, target = g.at[k, h, b, m4(a + 1), :, pl.ds(HALF // 2, HALF // 2)], a_dev(h, 3)
        elif k in WHOLE:
            way = 1 if i in (3, 11) else 3
            if i < 5:
                src = g.at[k, h, b]
            else:
                src = g.at[k, h, m4(b + 4 - way), pl.ds(0 if i == 11 else 2, 2)]
            target = b_dev(h, way)
        elif i < 11:
            j, way = (i - 3) // 2, (i - 3) % 2
            src, target = g.at[k, h, b, m4(a + j)], b_dev(h, 1 if way == 0 else 3)
        else:
            j = i - 11
            src = g.at[k, h, m4(b + (3 if j % 2 == 0 else 1)), m4(a + j)]
            target = b_dev(h, 1 if j % 2 == 0 else 3)
        return push(src, src, ag_s.at[k, h, i], ag_r.at[k, h, i], target)

    def step_z(k):
        for h in range(2):
            start(zg(k, h))

    def step_a(k):
        for h in range(2):
            if k:
                zg(k, h).wait_recv()
            for i in (0, 1) if k in WHOLE else (0, 1, 3, 4):
                start(ag(k, h, i))

    def step_b(k, i):
        j = (4 - A_STEPS[i]) % 4
        for h in range(2):
            ag(k, h, i).wait_recv()
            if i == 2:
                ag(k, h, 15).wait_recv()
            else:
                start(ag(k, h, 2 if i == 0 else 15))
            if k not in WHOLE:
                start(ag(k, h, 3 + 2 * j))
                start(ag(k, h, 4 + 2 * j))
            elif i == 2:
                start(ag(k, h, 3))
                start(ag(k, h, 4))

    def step_c(k, j):
        for h in range(2):
            ag(k, h, 3 + j if k in WHOLE else 3 + 2 * j + j % 2).wait_recv()
            start(ag(k, h, 11 + j))

    def step_w(k):
        for h in range(2):
            for j in range(0 if k in WHOLE else 4):
                ag(k, h, 3 + 2 * j + 1 - j % 2).wait_recv()
        for h in range(2):
            for j in range(2 if k in WHOLE else 4):
                ag(k, h, 11 + j).wait_recv()

    def xch(k, i):
        if i == 0:
            return push(part.at[k, 1 - core], cx.at[k], x_s.at[k, 0], x_r.at[k, 0], dev(dc=1))
        if i == 1:
            return push(q.at[k], zx.at[k], x_s.at[k, 1], x_r.at[k, 1], dev(dl=1))
        mine = codes.at[k, pl.ds(2 * core, 2)]
        return push(mine, mine, x_s.at[k, 2], x_r.at[k, 2], dev(dc=1))

    loaded = []

    def step_d(k):
        step_w(k)
        if not loaded:
            load_e.wait()
            load_d.wait()
            loaded.append(k)
        def body(n, c):
            at = pl.ds(pl.multiple_of(n * 256, 256), 256)
            r = jnp.dot(g[k, 0].reshape(256, HALF), we[cols[0], at], preferred_element_type=F32)
            lhs = jnp.concatenate([g[k, 1, :, i].reshape(64, HALF) for i in range(4)], axis=0)
            r = r + jnp.dot(lhs, we[cols[1], at], preferred_element_type=F32)
            part[k, :, :, at] = r.reshape(2, 128, 256)
            return c

        lax.fori_loop(0, 2, body, 0)
        start(xch(k, 0))

    def step_x(k):
        xch(k, 0).wait_recv()
        q[k] = part[k, core] + cx[k]
        start(xch(k, 1))

    def step_y(k):
        xch(k, 1).wait_recv()
        pre = q[k] + zx[k] + eb_ref[...]
        codes[k, pl.ds(2 * core, 2)] = jnp.maximum(pre, 0.0).astype(BF16).reshape(2, 4, ROWS, M)
        start(xch(k, 2))

    def wide(k):
        return HALF if k == 0 else SIDE

    def rs(k, h, i):
        a, b = ca[h], cb[h]
        at = pl.ds(0, wide(k))
        if i < 6:
            way = 1 if i % 2 == 0 else 3
            rows = pl.ds(2 if i in (1, 2, 5) else 0, 2)
            src = ob.at[k, h, m4(b + (2 if i < 2 else way)), rows, :, at]
            dst = r1.at[k, h, i, :, :, at] if i < 2 else r2.at[k, h, i % 2, rows, :, at]
            t = b_dev(h, way)
        elif i < 9:
            d = A_STEPS[i - 6]
            src, dst, t = asnd.at[k, h, m4(a + d), :, at], arcv.at[k, h, i - 6, :, at], a_dev(h, d)
        else:
            at = pl.ds(h * SIDE, SIDE)
            src, dst, t = zsnd.at[k, :, at], zrcv.at[k, :, at], dev(dz=OFF[k])
        return push(src, dst, rs_s.at[k, h, i], rs_r.at[k, h, i], t)

    def edge(k):
        return push(usnd.at[k], urcv.at[k], u_s.at[k], u_r.at[k], dev(dz=OFF[k]))

    def step_u(k):
        xch(k, 2).wait_recv()
        r = jnp.dot(codes[k].reshape(256, M), wd[:, pl.ds(2 * SIDE, EDGE)], preferred_element_type=F32)
        usnd[k] = r.reshape(4, 4, ROWS, EDGE).astype(BF16)
        start(edge(k))

    def tiles(width, step, body):
        def run(n, c):
            body(pl.multiple_of(n * step, step))
            return c

        lax.fori_loop(0, width // step, run, 0)

    def step_e(k, h):
        if k == 0 and h == 0:
            xch(k, 2).wait_recv()
        tile = 512 if k == 0 else 640

        def body(c0):
            at = pl.ds(c0, tile)
            r = jnp.dot(codes[k].reshape(256, M), wd[:, pl.ds(h * wide(k) + c0, tile)], preferred_element_type=F32)
            r = r.reshape(4, 4, ROWS, tile)
            if h == 0:
                full[k, 0, :, :, :, at] = r
                ob[k, 0, :, :, :, at] = r.astype(BF16)
            else:
                for i in range(4):
                    full[k, 1, :, i, :, at] = r[i]
                    ob[k, 1, :, i, :, at] = r[i].astype(BF16)

        tiles(wide(k), tile, body)
        if k == 0 and h == 1:
            at = pl.ds(HALF - EDGE, EDGE)
            for j in range(1, NK):
                edge(j).wait_recv()
            for i in range(4):
                r = full[0, 1, :, i, :, at]
                for j in range(1, NK):
                    r = r + urcv[j, i].astype(F32)
                full[0, 1, :, i, :, at] = r
                ob[0, 1, :, i, :, at] = r.astype(BF16)
        for i in range(4):
            start(rs(k, h, i))

    def step_f(k, h, w):
        rs(k, h, w).wait_recv()
        to = m4(cb[h] + (1 if w == 0 else 3))
        rows = pl.ds(0 if w == 0 else 2, 2)

        tile = 512 if k == 0 else 640

        def body(c0):
            at = pl.ds(c0, tile)
            got = r1[k, h, w, :, :, at].astype(F32)
            ob[k, h, to, rows, :, at] = (full[k, h, to, rows, :, at] + got).astype(BF16)

        tiles(wide(k), tile, body)
        start(rs(k, h, 4 + w))

    def step_g(k, h):
        for i in (2, 3, 4, 5):
            rs(k, h, i).wait_recv()
        b = cb[h]

        tile = 512 if k == 0 else 640

        def body(c0):
            at = pl.ds(c0, tile)
            got = r2[k, h, 0, :, :, at].astype(F32) + r2[k, h, 1, :, :, at].astype(F32)
            s = full[k, h, b, :, :, at] + got
            full[k, h, b, :, :, at] = s
            asnd[k, h, :, :, at] = s.astype(BF16)

        tiles(wide(k), tile, body)
        for i in (6, 7, 8):
            start(rs(k, h, i))

    def step_h(k, h):
        for i in (6, 7, 8):
            rs(k, h, i).wait_recv()
        at = pl.ds(0, wide(k))
        s = full[k, h, cb[h], ca[h], :, at]
        for i in range(3):
            s = s + arcv[k, h, i, :, at].astype(F32)
        if k == 0:
            acc[:, cols[h]] = s
        else:
            zsnd[k, :, pl.ds(h * SIDE, SIDE)] = s.astype(BF16)
            start(rs(k, h, 9))

    steps = dict(
        Z=step_z, A=step_a, B=step_b, C=step_c, D=step_d, X=step_x, Y=step_y, E=step_e, F=step_f, G=step_g, H=step_h,
        U=step_u,
    )
    for name in PROGRAM:
        steps[name[0]](*(int(v) for v in name[1:]))

    for k in range(1, NK):
        for h in range(2):
            rs(k, h, 9).wait_recv()
    at = pl.ds(0, 2 * SIDE)
    total = acc[:, at]
    for k in range(1, NK):
        total = total + zrcv[k, :, at].astype(F32)
    out_ref[:, at] = total
    at = pl.ds(2 * SIDE, EDGE)
    out_ref[:, at] = acc[:, at]
    for copy in sent:
        copy.wait_send()


def shards(streams, enc_weight, enc_bias, dec_weight, dec_bias):
    dma = pltpu.SemaphoreType.DMA
    any_space, vmem = pl.BlockSpec(memory_space=pl.ANY), pl.BlockSpec(memory_space=pltpu.VMEM)
    rows = pl.pallas_call(
        kernel,
        out_shape=jax.ShapeDtypeStruct((ROWS, D), F32),
        in_specs=[any_space, any_space, vmem, any_space],
        out_specs=vmem,
        scratch_shapes=[
            pltpu.VMEM((NK, 2, 4, 4, ROWS, HALF), BF16),
            pltpu.VMEM((D, M), BF16),
            pltpu.VMEM((M, D), BF16),
            pltpu.VMEM((NK, 2, 128, M), F32),
            pltpu.VMEM((NK, 128, M), F32),
            pltpu.VMEM((NK, 128, M), F32),
            pltpu.VMEM((NK, 128, M), F32),
            pltpu.VMEM((NK, 4, 4, ROWS, M), BF16),
            pltpu.VMEM((NK, 2, 4, 4, ROWS, HALF), F32),
            pltpu.VMEM((NK, 2, 4, 4, ROWS, HALF), BF16),
            pltpu.VMEM((NK, 2, 2, 2, ROWS, HALF), BF16),
            pltpu.VMEM((NK, 2, 2, 4, ROWS, HALF), BF16),
            pltpu.VMEM((NK, 2, 4, ROWS, HALF), BF16),
            pltpu.VMEM((NK, 2, 3, ROWS, HALF), BF16),
            pltpu.VMEM((NK, ROWS, D), BF16),
            pltpu.VMEM((NK, ROWS, D), BF16),
            pltpu.VMEM((NK, 4, 4, ROWS, EDGE), BF16),
            pltpu.VMEM((NK, 4, 4, ROWS, EDGE), BF16),
            pltpu.VMEM((ROWS, D), F32),
            dma((4,)),
            dma((NK, 2, 16)),
            dma((NK, 2, 16)),
            dma((NK, 2)),
            dma((NK, 2)),
            dma((NK, 3)),
            dma((NK, 3)),
            dma((NK, 2, 10)),
            dma((NK, 2, 10)),
            dma((NK,)),
            dma((NK,)),
        ],
        compiler_params=pltpu.CompilerParams(
            collective_id=1, has_side_effects=True, vmem_limit_bytes=61 * 1024 * 1024
        ),
        cost_estimate=pl.CostEstimate(flops=8 * 1024 * D * M, bytes_accessed=9 * 1024 * 1024, transcendentals=0),
        name="crosscoder",
    )(streams, enc_weight, enc_bias.reshape(1, M), dec_weight)
    return (rows + dec_bias)[None]


def solution(mesh):
    in_specs = (
        P("layer", "latent", None),
        P("layer", None, "latent"),
        P("latent"),
        P("layer", "latent", None),
        P("layer", None),
    )
    return jax.shard_map(
        shards, mesh=mesh, in_specs=in_specs, out_specs=P("layer", "latent", None), check_vma=False
    )
```

```python
import functools

import jax
import jax.numpy as jnp
from jax import lax
from jax.experimental import pallas as pl
from jax.experimental.pallas import tpu as pltpu
from jax.sharding import PartitionSpec as P

MESH = pl.DeviceIdType.MESH
F32, BF16 = jnp.float32, jnp.bfloat16
OFF = (0, 1, 3, 2)
NK = 4
ROWS, D, M, HALF = 16, 4096, 512, 2048
A_STEPS = (1, 3, 2)

PROGRAM = (
    "A0", "Z3", "B00", "B01", "Z2", "C00", "Z1", "A3", "C03", "B02", "A2", "B31",
    "C01", "A1", "B30", "C02", "C31", "B20", "B32", "B11", "C33", "C30", "D0", "C32",
    "X0", "B10", "C11", "B21", "C13", "B12", "D3", "C10", "B22", "C23", "Y0", "X3",
    "C12", "E00", "C20", "E01", "D1", "X1", "C21", "Y3", "C22", "E30", "E31", "F000",
    "F001", "D2", "F011", "F010", "X2", "Y1", "E10", "E11", "F300", "F311", "F310", "F301",
    "Y2", "E20", "E21", "F111", "F110", "G31", "G30", "F201", "F200", "F210", "F211", "F101",
    "F100", "H31", "G11", "G20", "H30", "G21", "G10", "H11", "H20", "G00", "G01", "H21",
    "H10", "H01", "H00",
)


def kernel(
    s_ref, we_hbm, eb_ref, wd_hbm, out_ref,
    g, we, wd, part, cx, q, zx, codes, full, ob, r1, r2, asnd, arcv, zsnd, zrcv, acc,
    lsem, ag_s, ag_r, zg_s, zg_r, x_s, x_r, rs_s, rs_r,
):
    lay, lat = lax.axis_index("layer"), lax.axis_index("latent")
    zlo, core = lay // 2, lay % 2
    x, y, z = lat // 16, (lat // 4) % 4, lat % 4
    m4 = lambda v: lax.rem(v + 8, 4)

    def dev(dx=0, dy=0, dz=0, dl=0, dc=0):
        return (
            lax.rem(zlo + dl, 2) * 2 + lax.rem(core + dc, 2),
            (m4(x + dx) * 4 + m4(y + dy)) * 4 + m4(z + dz),
        )

    def a_dev(h, d):
        return dev(dy=d) if h == 0 else dev(dx=d)

    def b_dev(h, d):
        return dev(dx=d) if h == 0 else dev(dy=d)

    ca = (y, x)
    cb = (x, y)
    cols = tuple(pl.ds(h * HALF, HALF) for h in range(2))

    def slot(buf, k, h, b, a):
        return buf.at[k, b, a, :, cols[h]] if h == 0 else buf.at[k, a, b, :, cols[h]]

    def span(buf, k, h, b, a0, n):
        return buf.at[k, b, pl.ds(a0, n), :, cols[h]] if h == 0 else buf.at[k, pl.ds(a0, n), b, :, cols[h]]

    def push(src, dst, ssem, rsem, target):
        return pltpu.make_async_remote_copy(
            src_ref=src, dst_ref=dst, send_sem=ssem, recv_sem=rsem, device_id=target, device_id_type=MESH
        )

    sent = []

    def start(copy):
        copy.start()
        sent.append(copy)

    load_s = pltpu.make_async_copy(s_ref.at[0], g.at[0, x, y], lsem.at[0])
    load_e = pltpu.make_async_copy(we_hbm.at[0], we, lsem.at[1])
    load_d = pltpu.make_async_copy(wd_hbm.at[0], wd, lsem.at[2])
    load_s.start()
    load_e.start()
    load_d.start()
    bar = pltpu.get_barrier_semaphore()
    partners = [dev(dx=d) for d in (1, 2, 3)] + [dev(dy=d) for d in (1, 2, 3)]
    partners += [dev(dz=d) for d in (1, 2, 3)] + [dev(dc=1), dev(dl=1)]
    for p in partners:
        pl.semaphore_signal(bar, inc=1, device_id=p, device_id_type=MESH)
    pl.semaphore_wait(bar, len(partners))
    load_s.wait()

    def zg(k):
        return push(g.at[0, x, y], g.at[k, x, y], zg_s.at[k], zg_r.at[k], dev(dz=4 - OFF[k]))

    def ag(k, h, i):
        a, b = ca[h], cb[h]
        if i < 2:
            src, target = slot(g, k, h, b, a), a_dev(h, A_STEPS[i])
        elif i == 2 or i == 15:
            from_a, w = (m4(a + 3), 0) if i == 2 else (m4(a + 1), 1)
            at = pl.ds(h * HALF + w * (HALF // 2), HALF // 2)
            src = g.at[k, b, from_a, :, at] if h == 0 else g.at[k, from_a, b, :, at]
            target = a_dev(h, 1 if i == 2 else 3)
        elif i < 11:
            j, way = (i - 3) // 2, (i - 3) % 2
            src, target = slot(g, k, h, b, m4(a + j)), b_dev(h, 1 if way == 0 else 3)
        else:
            j = i - 11
            src = slot(g, k, h, m4(b + (3 if j % 2 == 0 else 1)), m4(a + j))
            target = b_dev(h, 1 if j % 2 == 0 else 3)
        return push(src, src, ag_s.at[k, h, i], ag_r.at[k, h, i], target)

    def step_z(k):
        start(zg(k))

    def step_a(k):
        if k:
            zg(k).wait_recv()
        for h in range(2):
            for i in (0, 1, 3, 4):
                start(ag(k, h, i))

    def step_b(k, i):
        j = (4 - A_STEPS[i]) % 4
        for h in range(2):
            ag(k, h, i).wait_recv()
            if i == 2:
                ag(k, h, 15).wait_recv()
            else:
                start(ag(k, h, 2 if i == 0 else 15))
            start(ag(k, h, 3 + 2 * j))
            start(ag(k, h, 4 + 2 * j))

    def step_c(k, j):
        for h in range(2):
            ag(k, h, 3 + 2 * j + j % 2).wait_recv()
            start(ag(k, h, 11 + j))

    def step_w(k):
        for h in range(2):
            for j in range(4):
                ag(k, h, 3 + 2 * j + 1 - j % 2).wait_recv()
        for h in range(2):
            for j in range(4):
                ag(k, h, 11 + j).wait_recv()

    def xch(k, i):
        if i == 0:
            return push(part.at[k, 1 - core], cx.at[k], x_s.at[k, 0], x_r.at[k, 0], dev(dc=1))
        if i == 1:
            return push(q.at[k], zx.at[k], x_s.at[k, 1], x_r.at[k, 1], dev(dl=1))
        mine = codes.at[k, pl.ds(2 * core, 2)]
        return push(mine, mine, x_s.at[k, 2], x_r.at[k, 2], dev(dc=1))

    loaded = []

    def step_d(k):
        step_w(k)
        if not loaded:
            load_e.wait()
            load_d.wait()
            loaded.append(k)
        rows = g.at[k]

        def body(n, c):
            at = pl.ds(pl.multiple_of(n * 256, 256), 256)
            lhs = rows[...].reshape(256, D)
            r = jnp.dot(lhs, we[:, at], preferred_element_type=F32)
            part[k, :, :, at] = r.reshape(2, 128, 256)
            return c

        lax.fori_loop(0, 2, body, 0)
        start(xch(k, 0))

    def step_x(k):
        xch(k, 0).wait_recv()
        q[k] = part[k, core] + cx[k]
        start(xch(k, 1))

    def step_y(k):
        xch(k, 1).wait_recv()
        pre = q[k] + zx[k] + eb_ref[...]
        codes[k, pl.ds(2 * core, 2)] = jnp.maximum(pre, 0.0).astype(BF16).reshape(2, 4, ROWS, M)
        start(xch(k, 2))

    def rs(k, h, i):
        a, b = ca[h], cb[h]
        if i == 0:
            src, dst, t = span(ob, k, h, m4(b + 2), 0, 2), r1.at[k, h, 0], b_dev(h, 1)
        elif i == 1:
            src, dst, t = span(ob, k, h, m4(b + 2), 2, 2), r1.at[k, h, 1], b_dev(h, 3)
        elif i == 2:
            src, dst, t = span(ob, k, h, m4(b + 1), 2, 2), r2.at[k, h, 0, pl.ds(2, 2)], b_dev(h, 1)
        elif i == 3:
            src, dst, t = span(ob, k, h, m4(b + 3), 0, 2), r2.at[k, h, 1, pl.ds(0, 2)], b_dev(h, 3)
        elif i == 4:
            src, dst, t = span(ob, k, h, m4(b + 1), 0, 2), r2.at[k, h, 0, pl.ds(0, 2)], b_dev(h, 1)
        elif i == 5:
            src, dst, t = span(ob, k, h, m4(b + 3), 2, 2), r2.at[k, h, 1, pl.ds(2, 2)], b_dev(h, 3)
        elif i < 9:
            d = A_STEPS[i - 6]
            src, dst, t = asnd.at[k, h, m4(a + d)], arcv.at[k, h, i - 6], a_dev(h, d)
        else:
            src, dst, t = zsnd.at[k, :, cols[h]], zrcv.at[k, :, cols[h]], dev(dz=OFF[k])
        return push(src, dst, rs_s.at[k, h, i], rs_r.at[k, h, i], t)

    def step_e(k, h):
        if h == 0:
            xch(k, 2).wait_recv()

        def body(n, c):
            at = pl.ds(pl.multiple_of(h * HALF + n * 512, 512), 512)
            r = jnp.dot(codes[k].reshape(256, M), wd[:, at], preferred_element_type=F32)
            r = r.reshape(4, 4, ROWS, 512)
            full[k, :, :, :, at] = r
            ob[k, :, :, :, at] = r.astype(BF16)
            return c

        lax.fori_loop(0, HALF // 512, body, 0)
        for i in range(4):
            start(rs(k, h, i))

    def tiles(width, step, body):
        def run(n, c):
            body(pl.multiple_of(n * step, step))
            return c

        lax.fori_loop(0, width // step, run, 0)

    def step_f(k, h, w):
        rs(k, h, w).wait_recv()
        to = m4(cb[h] + (1 if w == 0 else 3))
        rows = pl.ds(0 if w == 0 else 2, 2)

        def body(c0):
            at = pl.ds(h * HALF + c0, 512)
            got = r1[k, h, w, :, :, pl.ds(c0, 512)].astype(F32)
            if h == 0:
                ob[k, to, rows, :, at] = (full[k, to, rows, :, at] + got).astype(BF16)
            else:
                ob[k, rows, to, :, at] = (full[k, rows, to, :, at] + got).astype(BF16)

        tiles(HALF, 512, body)
        start(rs(k, h, 4 + w))

    def step_g(k, h):
        for i in (2, 3, 4, 5):
            rs(k, h, i).wait_recv()
        b = cb[h]

        def body(c0):
            at = pl.ds(h * HALF + c0, 512)
            got = r2[k, h, 0, :, :, pl.ds(c0, 512)].astype(F32) + r2[k, h, 1, :, :, pl.ds(c0, 512)].astype(F32)
            if h == 0:
                s = full[k, b, :, :, at] + got
                full[k, b, :, :, at] = s
            else:
                s = full[k, :, b, :, at] + got
                full[k, :, b, :, at] = s
            asnd[k, h, :, :, pl.ds(c0, 512)] = s.astype(BF16)

        tiles(HALF, 512, body)
        for i in (6, 7, 8):
            start(rs(k, h, i))

    def step_h(k, h):
        for i in (6, 7, 8):
            rs(k, h, i).wait_recv()
        at = cols[h]
        s = full[k, x, y, :, at]
        for i in range(3):
            s = s + arcv[k, h, i].astype(F32)
        if k == 0:
            acc[:, at] = s
        else:
            zsnd[k, :, at] = s.astype(BF16)
            start(rs(k, h, 9))

    steps = dict(
        Z=step_z, A=step_a, B=step_b, C=step_c, D=step_d, X=step_x, Y=step_y, E=step_e, F=step_f, G=step_g, H=step_h
    )
    for name in PROGRAM:
        steps[name[0]](*(int(v) for v in name[1:]))

    for k in range(1, NK):
        for h in range(2):
            rs(k, h, 9).wait_recv()
    total = acc[...]
    for k in range(1, NK):
        total = total + zrcv[k].astype(F32)
    out_ref[...] = total
    for copy in sent:
        copy.wait_send()


def shards(streams, enc_weight, enc_bias, dec_weight, dec_bias):
    dma = pltpu.SemaphoreType.DMA
    any_space, vmem = pl.BlockSpec(memory_space=pl.ANY), pl.BlockSpec(memory_space=pltpu.VMEM)
    rows = pl.pallas_call(
        kernel,
        out_shape=jax.ShapeDtypeStruct((ROWS, D), F32),
        in_specs=[any_space, any_space, vmem, any_space],
        out_specs=vmem,
        scratch_shapes=[
            pltpu.VMEM((NK, 4, 4, ROWS, D), BF16),
            pltpu.VMEM((D, M), BF16),
            pltpu.VMEM((M, D), BF16),
            pltpu.VMEM((NK, 2, 128, M), F32),
            pltpu.VMEM((NK, 128, M), F32),
            pltpu.VMEM((NK, 128, M), F32),
            pltpu.VMEM((NK, 128, M), F32),
            pltpu.VMEM((NK, 4, 4, ROWS, M), BF16),
            pltpu.VMEM((4, 4, 4, ROWS, D), F32),
            pltpu.VMEM((NK, 4, 4, ROWS, D), BF16),
            pltpu.VMEM((NK, 2, 2, 2, ROWS, HALF), BF16),
            pltpu.VMEM((NK, 2, 2, 4, ROWS, HALF), BF16),
            pltpu.VMEM((NK, 2, 4, ROWS, HALF), BF16),
            pltpu.VMEM((NK, 2, 3, ROWS, HALF), BF16),
            pltpu.VMEM((NK, ROWS, D), BF16),
            pltpu.VMEM((NK, ROWS, D), BF16),
            pltpu.VMEM((ROWS, D), F32),
            dma((3,)),
            dma((NK, 2, 16)),
            dma((NK, 2, 16)),
            dma((NK,)),
            dma((NK,)),
            dma((NK, 3)),
            dma((NK, 3)),
            dma((NK, 2, 10)),
            dma((NK, 2, 10)),
        ],
        compiler_params=pltpu.CompilerParams(
            collective_id=1, has_side_effects=True, vmem_limit_bytes=61 * 1024 * 1024
        ),
        cost_estimate=pl.CostEstimate(flops=8 * 1024 * D * M, bytes_accessed=9 * 1024 * 1024, transcendentals=0),
        name="crosscoder",
    )(streams, enc_weight, enc_bias.reshape(1, M), dec_weight)
    return (rows + dec_bias)[None]


def solution(mesh):
    in_specs = (
        P("layer", "latent", None),
        P("layer", None, "latent"),
        P("latent"),
        P("layer", "latent", None),
        P("layer", None),
    )
    return jax.shard_map(
        shards, mesh=mesh, in_specs=in_specs, out_specs=P("layer", "latent", None), check_vma=False
    )
```

```python
import functools

import jax
import jax.numpy as jnp
from jax import lax
from jax.experimental import pallas as pl
from jax.experimental.pallas import tpu as pltpu
from jax.sharding import PartitionSpec as P

MESH = pl.DeviceIdType.MESH
F32, BF16 = jnp.float32, jnp.bfloat16
OFF = (0, 1, 3, 2)
NK = 4
ROWS, D, M, HALF = 16, 4096, 512, 2048
A_STEPS = (1, 3, 2)

PROGRAM = (
    "A0", "Z3", "B00", "B01", "Z2", "C00", "Z1", "A3", "C03", "B02", "A2", "B31",
    "C01", "A1", "B30", "C02", "C31", "B20", "B32", "B11", "C33", "C30", "D0", "C32",
    "X0", "B10", "C11", "B21", "C13", "B12", "D3", "C10", "B22", "C23", "Y0", "X3",
    "C12", "E00", "C20", "E01", "D1", "X1", "C21", "Y3", "C22", "E30", "E31", "F000",
    "F001", "D2", "F011", "F010", "X2", "Y1", "E10", "E11", "F300", "F311", "F310", "F301",
    "Y2", "E20", "E21", "F111", "F110", "G31", "G30", "F201", "F200", "F210", "F211", "F101",
    "F100", "H31", "G11", "G20", "H30", "G21", "G10", "H11", "H20", "G00", "G01", "H21",
    "H10", "H01", "H00",
)


def kernel(
    s_ref, we_hbm, eb_ref, wd_hbm, out_ref,
    g, we, wd, part, cx, q, zx, codes, full, ob, r1, r2, asnd, arcv, zsnd, zrcv, acc,
    lsem, ag_s, ag_r, zg_s, zg_r, x_s, x_r, rs_s, rs_r,
):
    lay, lat = lax.axis_index("layer"), lax.axis_index("latent")
    zlo, core = lay // 2, lay % 2
    x, y, z = lat // 16, (lat // 4) % 4, lat % 4
    m4 = lambda v: lax.rem(v + 8, 4)

    def dev(dx=0, dy=0, dz=0, dl=0, dc=0):
        return (
            lax.rem(zlo + dl, 2) * 2 + lax.rem(core + dc, 2),
            (m4(x + dx) * 4 + m4(y + dy)) * 4 + m4(z + dz),
        )

    def a_dev(h, d):
        return dev(dy=d) if h == 0 else dev(dx=d)

    def b_dev(h, d):
        return dev(dx=d) if h == 0 else dev(dy=d)

    ca = (y, x)
    cb = (x, y)
    cols = tuple(pl.ds(h * HALF, HALF) for h in range(2))

    def slot(buf, k, h, b, a):
        return buf.at[k, b, a, :, cols[h]] if h == 0 else buf.at[k, a, b, :, cols[h]]

    def span(buf, k, h, b, a0, n):
        return buf.at[k, b, pl.ds(a0, n), :, cols[h]] if h == 0 else buf.at[k, pl.ds(a0, n), b, :, cols[h]]

    def push(src, dst, ssem, rsem, target):
        return pltpu.make_async_remote_copy(
            src_ref=src, dst_ref=dst, send_sem=ssem, recv_sem=rsem, device_id=target, device_id_type=MESH
        )

    sent = []

    def start(copy):
        copy.start()
        sent.append(copy)

    load_s = pltpu.make_async_copy(s_ref.at[0], g.at[0, x, y], lsem.at[0])
    load_e = pltpu.make_async_copy(we_hbm.at[0], we, lsem.at[1])
    load_d = pltpu.make_async_copy(wd_hbm.at[0], wd, lsem.at[2])
    load_s.start()
    load_e.start()
    load_d.start()
    bar = pltpu.get_barrier_semaphore()
    partners = [dev(dx=d) for d in (1, 2, 3)] + [dev(dy=d) for d in (1, 2, 3)]
    partners += [dev(dz=d) for d in (1, 2, 3)] + [dev(dc=1), dev(dl=1)]
    for p in partners:
        pl.semaphore_signal(bar, inc=1, device_id=p, device_id_type=MESH)
    pl.semaphore_wait(bar, len(partners))
    load_s.wait()

    def zg(k):
        return push(g.at[0, x, y], g.at[k, x, y], zg_s.at[k], zg_r.at[k], dev(dz=4 - OFF[k]))

    def ag(k, h, i):
        a, b = ca[h], cb[h]
        if i < 2:
            src, target = slot(g, k, h, b, a), a_dev(h, A_STEPS[i])
        elif k == 0 and i == 2:
            src, target = slot(g, k, h, b, a), a_dev(h, 2)
        elif i == 2 or i == 15:
            from_a, w = (m4(a + 3), 0) if i == 2 else (m4(a + 1), 1)
            at = pl.ds(h * HALF + w * (HALF // 2), HALF // 2)
            src = g.at[k, b, from_a, :, at] if h == 0 else g.at[k, from_a, b, :, at]
            target = a_dev(h, 1 if i == 2 else 3)
        elif i < 11:
            j, way = (i - 3) // 2, (i - 3) % 2
            src, target = slot(g, k, h, b, m4(a + j)), b_dev(h, 1 if way == 0 else 3)
        else:
            j = i - 11
            src = slot(g, k, h, m4(b + (3 if j % 2 == 0 else 1)), m4(a + j))
            target = b_dev(h, 1 if j % 2 == 0 else 3)
        return push(src, src, ag_s.at[k, h, i], ag_r.at[k, h, i], target)

    def step_z(k):
        start(zg(k))

    def step_a(k):
        if k:
            zg(k).wait_recv()
        for h in range(2):
            for i in (0, 1, 3, 4, 2) if k == 0 else (0, 1, 3, 4):
                start(ag(k, h, i))

    def step_b(k, i):
        j = (4 - A_STEPS[i]) % 4
        for h in range(2):
            ag(k, h, i).wait_recv()
            if k and i == 2:
                ag(k, h, 15).wait_recv()
            elif k:
                start(ag(k, h, 2 if i == 0 else 15))
            start(ag(k, h, 3 + 2 * j))
            start(ag(k, h, 4 + 2 * j))

    def step_c(k, j):
        for h in range(2):
            ag(k, h, 3 + 2 * j + j % 2).wait_recv()
            start(ag(k, h, 11 + j))

    def step_w(k):
        for h in range(2):
            for j in range(4):
                ag(k, h, 3 + 2 * j + 1 - j % 2).wait_recv()
        for h in range(2):
            for j in range(4):
                ag(k, h, 11 + j).wait_recv()

    def xch(k, i):
        if i == 0:
            return push(part.at[k, 1 - core], cx.at[k], x_s.at[k, 0], x_r.at[k, 0], dev(dc=1))
        if i == 1:
            return push(q.at[k], zx.at[k], x_s.at[k, 1], x_r.at[k, 1], dev(dl=1))
        mine = codes.at[k, pl.ds(2 * core, 2)]
        return push(mine, mine, x_s.at[k, 2], x_r.at[k, 2], dev(dc=1))

    loaded = []

    def step_d(k):
        step_w(k)
        if not loaded:
            load_e.wait()
            load_d.wait()
            loaded.append(k)
        rows = g.at[k]

        def body(n, c):
            at = pl.ds(pl.multiple_of(n * 256, 256), 256)
            lhs = rows[...].reshape(256, D)
            r = jnp.dot(lhs, we[:, at], preferred_element_type=F32)
            part[k, :, :, at] = r.reshape(2, 128, 256)
            return c

        lax.fori_loop(0, 2, body, 0)
        start(xch(k, 0))

    def step_x(k):
        xch(k, 0).wait_recv()
        q[k] = part[k, core] + cx[k]
        start(xch(k, 1))

    def step_y(k):
        xch(k, 1).wait_recv()
        pre = q[k] + zx[k] + eb_ref[...]
        codes[k, pl.ds(2 * core, 2)] = jnp.maximum(pre, 0.0).astype(BF16).reshape(2, 4, ROWS, M)
        start(xch(k, 2))

    def rs(k, h, i):
        a, b = ca[h], cb[h]
        if i == 0:
            src, dst, t = span(ob, k, h, m4(b + 2), 0, 2), r1.at[k, h, 0], b_dev(h, 1)
        elif i == 1:
            src, dst, t = span(ob, k, h, m4(b + 2), 2, 2), r1.at[k, h, 1], b_dev(h, 3)
        elif i == 2:
            src, dst, t = span(ob, k, h, m4(b + 1), 2, 2), r2.at[k, h, 0, pl.ds(2, 2)], b_dev(h, 1)
        elif i == 3:
            src, dst, t = span(ob, k, h, m4(b + 3), 0, 2), r2.at[k, h, 1, pl.ds(0, 2)], b_dev(h, 3)
        elif i == 4:
            src, dst, t = span(ob, k, h, m4(b + 1), 0, 2), r2.at[k, h, 0, pl.ds(0, 2)], b_dev(h, 1)
        elif i == 5:
            src, dst, t = span(ob, k, h, m4(b + 3), 2, 2), r2.at[k, h, 1, pl.ds(2, 2)], b_dev(h, 3)
        elif i < 9:
            d = A_STEPS[i - 6]
            src, dst, t = asnd.at[k, h, m4(a + d)], arcv.at[k, h, i - 6], a_dev(h, d)
        else:
            src, dst, t = zsnd.at[k, :, cols[h]], zrcv.at[k, :, cols[h]], dev(dz=OFF[k])
        return push(src, dst, rs_s.at[k, h, i], rs_r.at[k, h, i], t)

    def step_e(k, h):
        if h == 0:
            xch(k, 2).wait_recv()

        def body(n, c):
            at = pl.ds(pl.multiple_of(h * HALF + n * 512, 512), 512)
            r = jnp.dot(codes[k].reshape(256, M), wd[:, at], preferred_element_type=F32)
            r = r.reshape(4, 4, ROWS, 512)
            full[k, :, :, :, at] = r
            ob[k, :, :, :, at] = r.astype(BF16)
            return c

        lax.fori_loop(0, HALF // 512, body, 0)
        for i in range(4):
            start(rs(k, h, i))

    def tiles(width, step, body):
        def run(n, c):
            body(pl.multiple_of(n * step, step))
            return c

        lax.fori_loop(0, width // step, run, 0)

    def step_f(k, h, w):
        rs(k, h, w).wait_recv()
        to = m4(cb[h] + (1 if w == 0 else 3))
        rows = pl.ds(0 if w == 0 else 2, 2)

        def body(c0):
            at = pl.ds(h * HALF + c0, 512)
            got = r1[k, h, w, :, :, pl.ds(c0, 512)].astype(F32)
            if h == 0:
                ob[k, to, rows, :, at] = (full[k, to, rows, :, at] + got).astype(BF16)
            else:
                ob[k, rows, to, :, at] = (full[k, rows, to, :, at] + got).astype(BF16)

        tiles(HALF, 512, body)
        start(rs(k, h, 4 + w))

    def step_g(k, h):
        for i in (2, 3, 4, 5):
            rs(k, h, i).wait_recv()
        b = cb[h]

        def body(c0):
            at = pl.ds(h * HALF + c0, 512)
            got = r2[k, h, 0, :, :, pl.ds(c0, 512)].astype(F32) + r2[k, h, 1, :, :, pl.ds(c0, 512)].astype(F32)
            if h == 0:
                s = full[k, b, :, :, at] + got
                full[k, b, :, :, at] = s
            else:
                s = full[k, :, b, :, at] + got
                full[k, :, b, :, at] = s
            asnd[k, h, :, :, pl.ds(c0, 512)] = s.astype(BF16)

        tiles(HALF, 512, body)
        for i in (6, 7, 8):
            start(rs(k, h, i))

    def step_h(k, h):
        for i in (6, 7, 8):
            rs(k, h, i).wait_recv()
        at = cols[h]
        s = full[k, x, y, :, at]
        for i in range(3):
            s = s + arcv[k, h, i].astype(F32)
        if k == 0:
            acc[:, at] = s
        else:
            zsnd[k, :, at] = s.astype(BF16)
            start(rs(k, h, 9))

    steps = dict(
        Z=step_z, A=step_a, B=step_b, C=step_c, D=step_d, X=step_x, Y=step_y, E=step_e, F=step_f, G=step_g, H=step_h
    )
    for name in PROGRAM:
        steps[name[0]](*(int(v) for v in name[1:]))

    for k in range(1, NK):
        for h in range(2):
            rs(k, h, 9).wait_recv()
    total = acc[...]
    for k in range(1, NK):
        total = total + zrcv[k].astype(F32)
    out_ref[...] = total
    for copy in sent:
        copy.wait_send()


def shards(streams, enc_weight, enc_bias, dec_weight, dec_bias):
    dma = pltpu.SemaphoreType.DMA
    any_space, vmem = pl.BlockSpec(memory_space=pl.ANY), pl.BlockSpec(memory_space=pltpu.VMEM)
    rows = pl.pallas_call(
        kernel,
        out_shape=jax.ShapeDtypeStruct((ROWS, D), F32),
        in_specs=[any_space, any_space, vmem, any_space],
        out_specs=vmem,
        scratch_shapes=[
            pltpu.VMEM((NK, 4, 4, ROWS, D), BF16),
            pltpu.VMEM((D, M), BF16),
            pltpu.VMEM((M, D), BF16),
            pltpu.VMEM((NK, 2, 128, M), F32),
            pltpu.VMEM((NK, 128, M), F32),
            pltpu.VMEM((NK, 128, M), F32),
            pltpu.VMEM((NK, 128, M), F32),
            pltpu.VMEM((NK, 4, 4, ROWS, M), BF16),
            pltpu.VMEM((4, 4, 4, ROWS, D), F32),
            pltpu.VMEM((NK, 4, 4, ROWS, D), BF16),
            pltpu.VMEM((NK, 2, 2, 2, ROWS, HALF), BF16),
            pltpu.VMEM((NK, 2, 2, 4, ROWS, HALF), BF16),
            pltpu.VMEM((NK, 2, 4, ROWS, HALF), BF16),
            pltpu.VMEM((NK, 2, 3, ROWS, HALF), BF16),
            pltpu.VMEM((NK, ROWS, D), BF16),
            pltpu.VMEM((NK, ROWS, D), BF16),
            pltpu.VMEM((ROWS, D), F32),
            dma((3,)),
            dma((NK, 2, 16)),
            dma((NK, 2, 16)),
            dma((NK,)),
            dma((NK,)),
            dma((NK, 3)),
            dma((NK, 3)),
            dma((NK, 2, 10)),
            dma((NK, 2, 10)),
        ],
        compiler_params=pltpu.CompilerParams(
            collective_id=1, has_side_effects=True, vmem_limit_bytes=61 * 1024 * 1024
        ),
        cost_estimate=pl.CostEstimate(flops=8 * 1024 * D * M, bytes_accessed=9 * 1024 * 1024, transcendentals=0),
        name="crosscoder",
    )(streams, enc_weight, enc_bias.reshape(1, M), dec_weight)
    return (rows + dec_bias)[None]


def solution(mesh):
    in_specs = (
        P("layer", "latent", None),
        P("layer", None, "latent"),
        P("latent"),
        P("layer", "latent", None),
        P("layer", None),
    )
    return jax.shard_map(
        shards, mesh=mesh, in_specs=in_specs, out_specs=P("layer", "latent", None), check_vma=False
    )
```

```python
import functools

import jax
import jax.numpy as jnp
from jax import lax
from jax.experimental import pallas as pl
from jax.experimental.pallas import tpu as pltpu
from jax.sharding import PartitionSpec as P

MESH = pl.DeviceIdType.MESH
F32, BF16 = jnp.float32, jnp.bfloat16
OFF = (0, 1, 3, 2)
NK = 4
ROWS, D, M, HALF = 16, 4096, 512, 2048
A_STEPS = (1, 3, 2)

PROGRAM = (
    "A0", "Z3", "B00", "B01", "Z2", "C00", "Z1", "A3", "C03", "B02", "A2", "B31",
    "C01", "A1", "B30", "C02", "C31", "B20", "B32", "B11", "C33", "C30", "D0", "C32",
    "X0", "B10", "C11", "B21", "C13", "B12", "D3", "C10", "B22", "C23", "Y0", "X3",
    "C12", "E00", "C20", "E01", "D1", "X1", "C21", "Y3", "C22", "E30", "E31", "F000",
    "F001", "D2", "F011", "F010", "X2", "Y1", "E10", "E11", "F300", "F311", "F310", "F301",
    "Y2", "E20", "E21", "F111", "F110", "G31", "G30", "F201", "F200", "F210", "F211", "F101",
    "F100", "H31", "G11", "G20", "H30", "G21", "G10", "H11", "H20", "G00", "G01", "H21",
    "H10", "H01", "H00",
)


def kernel(
    s_ref, we_hbm, eb_ref, wd_hbm, out_ref,
    g, we, wd, part, cx, q, zx, codes, full, ob, r1, r2, asnd, arcv, zsnd, zrcv, acc,
    lsem, ag_s, ag_r, zg_s, zg_r, x_s, x_r, rs_s, rs_r,
):
    lay, lat = lax.axis_index("layer"), lax.axis_index("latent")
    zlo, core = lay // 2, lay % 2
    x, y, z = lat // 16, (lat // 4) % 4, lat % 4
    m4 = lambda v: lax.rem(v + 8, 4)

    def dev(dx=0, dy=0, dz=0, dl=0, dc=0):
        return (
            lax.rem(zlo + dl, 2) * 2 + lax.rem(core + dc, 2),
            (m4(x + dx) * 4 + m4(y + dy)) * 4 + m4(z + dz),
        )

    def a_dev(h, d):
        return dev(dy=d) if h == 0 else dev(dx=d)

    def b_dev(h, d):
        return dev(dx=d) if h == 0 else dev(dy=d)

    ca = (y, x)
    cb = (x, y)
    cols = tuple(pl.ds(h * HALF, HALF) for h in range(2))

    def slot(buf, k, h, b, a):
        return buf.at[k, b, a, :, cols[h]] if h == 0 else buf.at[k, a, b, :, cols[h]]

    def span(buf, k, h, b, a0, n):
        return buf.at[k, b, pl.ds(a0, n), :, cols[h]] if h == 0 else buf.at[k, pl.ds(a0, n), b, :, cols[h]]

    def push(src, dst, ssem, rsem, target):
        return pltpu.make_async_remote_copy(
            src_ref=src, dst_ref=dst, send_sem=ssem, recv_sem=rsem, device_id=target, device_id_type=MESH
        )

    sent = []

    def start(copy):
        copy.start()
        sent.append(copy)

    load_s = pltpu.make_async_copy(s_ref.at[0], g.at[0, x, y], lsem.at[0])
    load_e = pltpu.make_async_copy(we_hbm.at[0], we, lsem.at[1])
    load_d = pltpu.make_async_copy(wd_hbm.at[0], wd, lsem.at[2])
    load_s.start()
    load_e.start()
    load_d.start()
    bar = pltpu.get_barrier_semaphore()
    partners = [dev(dx=d) for d in (1, 2, 3)] + [dev(dy=d) for d in (1, 2, 3)]
    partners += [dev(dz=d) for d in (1, 2, 3)] + [dev(dc=1), dev(dl=1)]
    for p in partners:
        pl.semaphore_signal(bar, inc=1, device_id=p, device_id_type=MESH)
    pl.semaphore_wait(bar, len(partners))
    load_s.wait()

    def zg(k):
        return push(g.at[0, x, y], g.at[k, x, y], zg_s.at[k], zg_r.at[k], dev(dz=4 - OFF[k]))

    def ag(k, h, i):
        a, b = ca[h], cb[h]
        if i < 2:
            src, target = slot(g, k, h, b, a), a_dev(h, A_STEPS[i])
        elif k == 0 and i == 2:
            src, target = slot(g, k, h, b, a), a_dev(h, 2)
        elif i == 2 or i == 15:
            from_a, w = (m4(a + 3), 0) if i == 2 else (m4(a + 1), 1)
            at = pl.ds(h * HALF + w * (HALF // 2), HALF // 2)
            src = g.at[k, b, from_a, :, at] if h == 0 else g.at[k, from_a, b, :, at]
            target = a_dev(h, 1 if i == 2 else 3)
        elif i < 11:
            j, way = (i - 3) // 2, (i - 3) % 2
            src, target = slot(g, k, h, b, m4(a + j)), b_dev(h, 1 if way == 0 else 3)
        else:
            j = i - 11
            src = slot(g, k, h, m4(b + (3 if j % 2 == 0 else 1)), m4(a + j))
            target = b_dev(h, 1 if j % 2 == 0 else 3)
        return push(src, src, ag_s.at[k, h, i], ag_r.at[k, h, i], target)

    def step_z(k):
        start(zg(k))

    def step_a(k):
        if k:
            zg(k).wait_recv()
        for h in range(2):
            for i in (0, 1, 3, 4, 2) if k == 0 else (0, 1, 3, 4):
                start(ag(k, h, i))

    def step_b(k, i):
        j = (4 - A_STEPS[i]) % 4
        for h in range(2):
            ag(k, h, i).wait_recv()
            if k and i == 2:
                ag(k, h, 15).wait_recv()
            elif k:
                start(ag(k, h, 2 if i == 0 else 15))
            start(ag(k, h, 3 + 2 * j))
            start(ag(k, h, 4 + 2 * j))

    def step_c(k, j):
        for h in range(2):
            ag(k, h, 3 + 2 * j + j % 2).wait_recv()
            start(ag(k, h, 11 + j))

    def step_w(k):
        for h in range(2):
            for j in range(4):
                ag(k, h, 3 + 2 * j + 1 - j % 2).wait_recv()
        for h in range(2):
            for j in range(4):
                ag(k, h, 11 + j).wait_recv()

    def xch(k, i):
        if i == 0:
            return push(part.at[k, 1 - core], cx.at[k], x_s.at[k, 0], x_r.at[k, 0], dev(dc=1))
        if i == 1:
            return push(q.at[k], zx.at[k], x_s.at[k, 1], x_r.at[k, 1], dev(dl=1))
        mine = codes.at[k, pl.ds(2 * core, 2)]
        return push(mine, mine, x_s.at[k, 2], x_r.at[k, 2], dev(dc=1))

    loaded = []

    def step_d(k):
        step_w(k)
        if not loaded:
            load_e.wait()
            load_d.wait()
            loaded.append(k)
        rows = g.at[k]

        def body(n, c):
            at = pl.ds(pl.multiple_of(n * 256, 256), 256)
            lhs = rows[...].reshape(256, D)
            r = jnp.dot(lhs, we[:, at], preferred_element_type=F32)
            part[k, :, :, at] = r.reshape(2, 128, 256)
            return c

        lax.fori_loop(0, 2, body, 0)
        start(xch(k, 0))

    def step_x(k):
        xch(k, 0).wait_recv()
        q[k] = part[k, core] + cx[k]
        start(xch(k, 1))

    def step_y(k):
        xch(k, 1).wait_recv()
        pre = q[k] + zx[k] + eb_ref[...]
        codes[k, pl.ds(2 * core, 2)] = jnp.maximum(pre, 0.0).astype(BF16).reshape(2, 4, ROWS, M)
        start(xch(k, 2))

    def rs(k, h, i):
        a, b = ca[h], cb[h]
        if i == 0:
            src, dst, t = span(ob, k, h, m4(b + 2), 0, 2), r1.at[k, h, 0], b_dev(h, 1)
        elif i == 1:
            src, dst, t = span(ob, k, h, m4(b + 2), 2, 2), r1.at[k, h, 1], b_dev(h, 3)
        elif i == 2:
            src, dst, t = span(ob, k, h, m4(b + 1), 2, 2), r2.at[k, h, 0, pl.ds(2, 2)], b_dev(h, 1)
        elif i == 3:
            src, dst, t = span(ob, k, h, m4(b + 3), 0, 2), r2.at[k, h, 1, pl.ds(0, 2)], b_dev(h, 3)
        elif i == 4:
            src, dst, t = span(ob, k, h, m4(b + 1), 0, 2), r2.at[k, h, 0, pl.ds(0, 2)], b_dev(h, 1)
        elif i == 5:
            src, dst, t = span(ob, k, h, m4(b + 3), 2, 2), r2.at[k, h, 1, pl.ds(2, 2)], b_dev(h, 3)
        elif i < 9:
            d = A_STEPS[i - 6]
            src, dst, t = asnd.at[k, h, m4(a + d)], arcv.at[k, h, i - 6], a_dev(h, d)
        else:
            src, dst, t = zsnd.at[k, :, cols[h]], zrcv.at[k, :, cols[h]], dev(dz=OFF[k])
        return push(src, dst, rs_s.at[k, h, i], rs_r.at[k, h, i], t)

    def step_e(k, h):
        if h == 0:
            xch(k, 2).wait_recv()

        def body(n, c):
            at = pl.ds(pl.multiple_of(h * HALF + n * 512, 512), 512)
            r = jnp.dot(codes[k].reshape(256, M), wd[:, at], preferred_element_type=F32)
            r = r.reshape(4, 4, ROWS, 512)
            full[k, :, :, :, at] = r
            ob[k, :, :, :, at] = r.astype(BF16)
            return c

        lax.fori_loop(0, HALF // 512, body, 0)
        for i in range(4):
            start(rs(k, h, i))

    def tiles(width, step, body):
        def run(n, c):
            body(pl.multiple_of(n * step, step))
            return c

        lax.fori_loop(0, width // step, run, 0)

    def step_f(k, h, w):
        rs(k, h, w).wait_recv()
        to = m4(cb[h] + (1 if w == 0 else 3))
        rows = pl.ds(0 if w == 0 else 2, 2)

        def body(c0):
            at = pl.ds(h * HALF + c0, 1024)
            got = r1[k, h, w, :, :, pl.ds(c0, 1024)].astype(F32)
            if h == 0:
                ob[k, to, rows, :, at] = (full[k, to, rows, :, at] + got).astype(BF16)
            else:
                ob[k, rows, to, :, at] = (full[k, rows, to, :, at] + got).astype(BF16)

        tiles(HALF, 1024, body)
        start(rs(k, h, 4 + w))

    def step_g(k, h):
        for i in (2, 3, 4, 5):
            rs(k, h, i).wait_recv()
        b = cb[h]

        def body(c0):
            at = pl.ds(h * HALF + c0, 1024)
            got = r2[k, h, 0, :, :, pl.ds(c0, 1024)].astype(F32) + r2[k, h, 1, :, :, pl.ds(c0, 1024)].astype(F32)
            if h == 0:
                s = full[k, b, :, :, at] + got
                full[k, b, :, :, at] = s
            else:
                s = full[k, :, b, :, at] + got
                full[k, :, b, :, at] = s
            asnd[k, h, :, :, pl.ds(c0, 1024)] = s.astype(BF16)

        tiles(HALF, 1024, body)
        for i in (6, 7, 8):
            start(rs(k, h, i))

    def step_h(k, h):
        for i in (6, 7, 8):
            rs(k, h, i).wait_recv()
        at = cols[h]
        s = full[k, x, y, :, at]
        for i in range(3):
            s = s + arcv[k, h, i].astype(F32)
        if k == 0:
            acc[:, at] = s
        else:
            zsnd[k, :, at] = s.astype(BF16)
            start(rs(k, h, 9))

    steps = dict(
        Z=step_z, A=step_a, B=step_b, C=step_c, D=step_d, X=step_x, Y=step_y, E=step_e, F=step_f, G=step_g, H=step_h
    )
    for name in PROGRAM:
        steps[name[0]](*(int(v) for v in name[1:]))

    for k in range(1, NK):
        for h in range(2):
            rs(k, h, 9).wait_recv()
    total = acc[...]
    for k in range(1, NK):
        total = total + zrcv[k].astype(F32)
    out_ref[...] = total
    for copy in sent:
        copy.wait_send()


def shards(streams, enc_weight, enc_bias, dec_weight, dec_bias):
    dma = pltpu.SemaphoreType.DMA
    any_space, vmem = pl.BlockSpec(memory_space=pl.ANY), pl.BlockSpec(memory_space=pltpu.VMEM)
    rows = pl.pallas_call(
        kernel,
        out_shape=jax.ShapeDtypeStruct((ROWS, D), F32),
        in_specs=[any_space, any_space, vmem, any_space],
        out_specs=vmem,
        scratch_shapes=[
            pltpu.VMEM((NK, 4, 4, ROWS, D), BF16),
            pltpu.VMEM((D, M), BF16),
            pltpu.VMEM((M, D), BF16),
            pltpu.VMEM((NK, 2, 128, M), F32),
            pltpu.VMEM((NK, 128, M), F32),
            pltpu.VMEM((NK, 128, M), F32),
            pltpu.VMEM((NK, 128, M), F32),
            pltpu.VMEM((NK, 4, 4, ROWS, M), BF16),
            pltpu.VMEM((4, 4, 4, ROWS, D), F32),
            pltpu.VMEM((NK, 4, 4, ROWS, D), BF16),
            pltpu.VMEM((NK, 2, 2, 2, ROWS, HALF), BF16),
            pltpu.VMEM((NK, 2, 2, 4, ROWS, HALF), BF16),
            pltpu.VMEM((NK, 2, 4, ROWS, HALF), BF16),
            pltpu.VMEM((NK, 2, 3, ROWS, HALF), BF16),
            pltpu.VMEM((NK, ROWS, D), BF16),
            pltpu.VMEM((NK, ROWS, D), BF16),
            pltpu.VMEM((ROWS, D), F32),
            dma((3,)),
            dma((NK, 2, 16)),
            dma((NK, 2, 16)),
            dma((NK,)),
            dma((NK,)),
            dma((NK, 3)),
            dma((NK, 3)),
            dma((NK, 2, 10)),
            dma((NK, 2, 10)),
        ],
        compiler_params=pltpu.CompilerParams(
            collective_id=1, has_side_effects=True, vmem_limit_bytes=61 * 1024 * 1024
        ),
        cost_estimate=pl.CostEstimate(flops=8 * 1024 * D * M, bytes_accessed=9 * 1024 * 1024, transcendentals=0),
        name="crosscoder",
    )(streams, enc_weight, enc_bias.reshape(1, M), dec_weight)
    return (rows + dec_bias)[None]


def solution(mesh):
    in_specs = (
        P("layer", "latent", None),
        P("layer", None, "latent"),
        P("latent"),
        P("layer", "latent", None),
        P("layer", None),
    )
    return jax.shard_map(
        shards, mesh=mesh, in_specs=in_specs, out_specs=P("layer", "latent", None), check_vma=False
    )
```

```python
import functools

import jax
import jax.numpy as jnp
from jax import lax
from jax.experimental import pallas as pl
from jax.experimental.pallas import tpu as pltpu
from jax.sharding import PartitionSpec as P

MESH = pl.DeviceIdType.MESH
F32, BF16 = jnp.float32, jnp.bfloat16
OFF = (0, 1, 3, 2)
NK = 4
ROWS, D, M, HALF = 16, 4096, 512, 2048
A_STEPS = (1, 3, 2)

PROGRAM = (
    "A0", "Z3", "B00", "B01", "Z2", "C00", "Z1", "A3", "C03", "B02", "A2", "B31",
    "C01", "A1", "B30", "C02", "C31", "B20", "B32", "B11", "C33", "C30", "D0", "C32",
    "X0", "B10", "C11", "B21", "C13", "B12", "D3", "C10", "B22", "C23", "Y0", "X3",
    "C12", "E00", "C20", "E01", "D1", "X1", "C21", "Y3", "C22", "E30", "E31", "F000",
    "F001", "D2", "F011", "F010", "X2", "Y1", "E10", "E11", "F300", "F311", "F310", "F301",
    "Y2", "E20", "E21", "F111", "F110", "G31", "G30", "F201", "F200", "F210", "F211", "F101",
    "F100", "H31", "G11", "G20", "H30", "G21", "G10", "H11", "H20", "G00", "G01", "H21",
    "H10", "H01", "H00",
)


def kernel(
    s_ref, we_hbm, eb_ref, wd_hbm, out_ref,
    g, we, wd, part, cx, q, zx, codes, full, ob, r1, r2, asnd, arcv, zsnd, zrcv, acc,
    lsem, ag_s, ag_r, zg_s, zg_r, x_s, x_r, rs_s, rs_r,
):
    lay, lat = lax.axis_index("layer"), lax.axis_index("latent")
    zlo, core = lay // 2, lay % 2
    x, y, z = lat // 16, (lat // 4) % 4, lat % 4
    m4 = lambda v: lax.rem(v + 8, 4)

    def dev(dx=0, dy=0, dz=0, dl=0, dc=0):
        return (
            lax.rem(zlo + dl, 2) * 2 + lax.rem(core + dc, 2),
            (m4(x + dx) * 4 + m4(y + dy)) * 4 + m4(z + dz),
        )

    def a_dev(h, d):
        return dev(dy=d) if h == 0 else dev(dx=d)

    def b_dev(h, d):
        return dev(dx=d) if h == 0 else dev(dy=d)

    ca = (y, x)
    cb = (x, y)
    cols = tuple(pl.ds(h * HALF, HALF) for h in range(2))

    def slot(buf, k, h, b, a):
        return buf.at[k, b, a, :, cols[h]] if h == 0 else buf.at[k, a, b, :, cols[h]]

    def span(buf, k, h, b, a0, n):
        return buf.at[k, b, pl.ds(a0, n), :, cols[h]] if h == 0 else buf.at[k, pl.ds(a0, n), b, :, cols[h]]

    def push(src, dst, ssem, rsem, target):
        return pltpu.make_async_remote_copy(
            src_ref=src, dst_ref=dst, send_sem=ssem, recv_sem=rsem, device_id=target, device_id_type=MESH
        )

    sent = []

    def start(copy):
        copy.start()
        sent.append(copy)

    load_s = pltpu.make_async_copy(s_ref.at[0], g.at[0, x, y], lsem.at[0])
    load_e = pltpu.make_async_copy(we_hbm.at[0], we, lsem.at[1])
    load_d = pltpu.make_async_copy(wd_hbm.at[0], wd, lsem.at[2])
    load_s.start()
    load_e.start()
    load_d.start()
    bar = pltpu.get_barrier_semaphore()
    partners = [dev(dx=d) for d in (1, 2, 3)] + [dev(dy=d) for d in (1, 2, 3)]
    partners += [dev(dz=d) for d in (1, 2, 3)] + [dev(dc=1), dev(dl=1)]
    for p in partners:
        pl.semaphore_signal(bar, inc=1, device_id=p, device_id_type=MESH)
    pl.semaphore_wait(bar, len(partners))
    load_s.wait()

    def zg(k):
        return push(g.at[0, x, y], g.at[k, x, y], zg_s.at[k], zg_r.at[k], dev(dz=4 - OFF[k]))

    def ag(k, h, i):
        a, b = ca[h], cb[h]
        if i < 2:
            src, target = slot(g, k, h, b, a), a_dev(h, A_STEPS[i])
        elif k == 0 and i == 2:
            src, target = slot(g, k, h, b, a), a_dev(h, 2)
        elif i == 2 or i == 15:
            from_a, w = (m4(a + 3), 0) if i == 2 else (m4(a + 1), 1)
            at = pl.ds(h * HALF + w * (HALF // 2), HALF // 2)
            src = g.at[k, b, from_a, :, at] if h == 0 else g.at[k, from_a, b, :, at]
            target = a_dev(h, 1 if i == 2 else 3)
        elif i < 11:
            j, way = (i - 3) // 2, (i - 3) % 2
            src, target = slot(g, k, h, b, m4(a + j)), b_dev(h, 1 if way == 0 else 3)
        else:
            j = i - 11
            src = slot(g, k, h, m4(b + (3 if j % 2 == 0 else 1)), m4(a + j))
            target = b_dev(h, 1 if j % 2 == 0 else 3)
        return push(src, src, ag_s.at[k, h, i], ag_r.at[k, h, i], target)

    def step_z(k):
        start(zg(k))

    def step_a(k):
        if k:
            zg(k).wait_recv()
        for h in range(2):
            for i in (0, 1, 3, 4, 2) if k == 0 else (0, 1, 3, 4):
                start(ag(k, h, i))

    def step_b(k, i):
        j = (4 - A_STEPS[i]) % 4
        for h in range(2):
            ag(k, h, i).wait_recv()
            if k and i == 2:
                ag(k, h, 15).wait_recv()
            elif k:
                start(ag(k, h, 2 if i == 0 else 15))
            start(ag(k, h, 3 + 2 * j))
            start(ag(k, h, 4 + 2 * j))

    def step_c(k, j):
        for h in range(2):
            ag(k, h, 3 + 2 * j + j % 2).wait_recv()
            start(ag(k, h, 11 + j))

    def step_w(k):
        for h in range(2):
            for j in range(4):
                ag(k, h, 3 + 2 * j + 1 - j % 2).wait_recv()
        for h in range(2):
            for j in range(4):
                ag(k, h, 11 + j).wait_recv()

    def xch(k, i):
        if i == 0:
            return push(part.at[k, 1 - core], cx.at[k], x_s.at[k, 0], x_r.at[k, 0], dev(dc=1))
        if i == 1:
            return push(q.at[k], zx.at[k], x_s.at[k, 1], x_r.at[k, 1], dev(dl=1))
        mine = codes.at[k, pl.ds(2 * core, 2)]
        return push(mine, mine, x_s.at[k, 2], x_r.at[k, 2], dev(dc=1))

    loaded = []

    def step_d(k):
        step_w(k)
        if not loaded:
            load_e.wait()
            load_d.wait()
            loaded.append(k)
        rows = g.at[k]

        def body(n, c):
            at = pl.ds(pl.multiple_of(n * 256, 256), 256)
            lhs = rows[...].reshape(256, D)
            r = jnp.dot(lhs, we[:, at], preferred_element_type=F32)
            part[k, :, :, at] = r.reshape(2, 128, 256)
            return c

        lax.fori_loop(0, 2, body, 0)
        start(xch(k, 0))

    def step_x(k):
        xch(k, 0).wait_recv()
        q[k] = part[k, core] + cx[k]
        start(xch(k, 1))

    def step_y(k):
        xch(k, 1).wait_recv()
        pre = q[k] + zx[k] + eb_ref[...]
        codes[k, pl.ds(2 * core, 2)] = jnp.maximum(pre, 0.0).astype(BF16).reshape(2, 4, ROWS, M)
        start(xch(k, 2))

    def rs(k, h, i):
        a, b = ca[h], cb[h]
        if i == 0:
            src, dst, t = span(ob, k, h, m4(b + 2), 0, 2), r1.at[k, h, 0], b_dev(h, 1)
        elif i == 1:
            src, dst, t = span(ob, k, h, m4(b + 2), 2, 2), r1.at[k, h, 1], b_dev(h, 3)
        elif i == 2:
            src, dst, t = span(ob, k, h, m4(b + 1), 2, 2), r2.at[k, h, 0, pl.ds(2, 2)], b_dev(h, 1)
        elif i == 3:
            src, dst, t = span(ob, k, h, m4(b + 3), 0, 2), r2.at[k, h, 1, pl.ds(0, 2)], b_dev(h, 3)
        elif i == 4:
            src, dst, t = span(ob, k, h, m4(b + 1), 0, 2), r2.at[k, h, 0, pl.ds(0, 2)], b_dev(h, 1)
        elif i == 5:
            src, dst, t = span(ob, k, h, m4(b + 3), 2, 2), r2.at[k, h, 1, pl.ds(2, 2)], b_dev(h, 3)
        elif i < 9:
            d = A_STEPS[i - 6]
            src, dst, t = asnd.at[k, h, m4(a + d)], arcv.at[k, h, i - 6], a_dev(h, d)
        else:
            src, dst, t = zsnd.at[k, :, cols[h]], zrcv.at[k, :, cols[h]], dev(dz=OFF[k])
        return push(src, dst, rs_s.at[k, h, i], rs_r.at[k, h, i], t)

    def step_e(k, h):
        if h == 0:
            xch(k, 2).wait_recv()

        def body(n, c):
            at = pl.ds(pl.multiple_of(h * HALF + n * 1024, 1024), 1024)
            r = jnp.dot(codes[k].reshape(256, M), wd[:, at], preferred_element_type=F32)
            r = r.reshape(4, 4, ROWS, 1024)
            full[k, :, :, :, at] = r
            ob[k, :, :, :, at] = r.astype(BF16)
            return c

        lax.fori_loop(0, HALF // 1024, body, 0)
        for i in range(4):
            start(rs(k, h, i))

    def tiles(width, step, body):
        def run(n, c):
            body(pl.multiple_of(n * step, step))
            return c

        lax.fori_loop(0, width // step, run, 0)

    def step_f(k, h, w):
        rs(k, h, w).wait_recv()
        to = m4(cb[h] + (1 if w == 0 else 3))
        rows = pl.ds(0 if w == 0 else 2, 2)

        def body(c0):
            at = pl.ds(h * HALF + c0, 512)
            got = r1[k, h, w, :, :, pl.ds(c0, 512)].astype(F32)
            if h == 0:
                ob[k, to, rows, :, at] = (full[k, to, rows, :, at] + got).astype(BF16)
            else:
                ob[k, rows, to, :, at] = (full[k, rows, to, :, at] + got).astype(BF16)

        tiles(HALF, 512, body)
        start(rs(k, h, 4 + w))

    def step_g(k, h):
        for i in (2, 3, 4, 5):
            rs(k, h, i).wait_recv()
        b = cb[h]

        def body(c0):
            at = pl.ds(h * HALF + c0, 512)
            got = r2[k, h, 0, :, :, pl.ds(c0, 512)].astype(F32) + r2[k, h, 1, :, :, pl.ds(c0, 512)].astype(F32)
            if h == 0:
                s = full[k, b, :, :, at] + got
                full[k, b, :, :, at] = s
            else:
                s = full[k, :, b, :, at] + got
                full[k, :, b, :, at] = s
            asnd[k, h, :, :, pl.ds(c0, 512)] = s.astype(BF16)

        tiles(HALF, 512, body)
        for i in (6, 7, 8):
            start(rs(k, h, i))

    def step_h(k, h):
        for i in (6, 7, 8):
            rs(k, h, i).wait_recv()
        at = cols[h]
        s = full[k, x, y, :, at]
        for i in range(3):
            s = s + arcv[k, h, i].astype(F32)
        if k == 0:
            acc[:, at] = s
        else:
            zsnd[k, :, at] = s.astype(BF16)
            start(rs(k, h, 9))

    steps = dict(
        Z=step_z, A=step_a, B=step_b, C=step_c, D=step_d, X=step_x, Y=step_y, E=step_e, F=step_f, G=step_g, H=step_h
    )
    for name in PROGRAM:
        steps[name[0]](*(int(v) for v in name[1:]))

    for k in range(1, NK):
        for h in range(2):
            rs(k, h, 9).wait_recv()
    total = acc[...]
    for k in range(1, NK):
        total = total + zrcv[k].astype(F32)
    out_ref[...] = total
    for copy in sent:
        copy.wait_send()


def shards(streams, enc_weight, enc_bias, dec_weight, dec_bias):
    dma = pltpu.SemaphoreType.DMA
    any_space, vmem = pl.BlockSpec(memory_space=pl.ANY), pl.BlockSpec(memory_space=pltpu.VMEM)
    rows = pl.pallas_call(
        kernel,
        out_shape=jax.ShapeDtypeStruct((ROWS, D), F32),
        in_specs=[any_space, any_space, vmem, any_space],
        out_specs=vmem,
        scratch_shapes=[
            pltpu.VMEM((NK, 4, 4, ROWS, D), BF16),
            pltpu.VMEM((D, M), BF16),
            pltpu.VMEM((M, D), BF16),
            pltpu.VMEM((NK, 2, 128, M), F32),
            pltpu.VMEM((NK, 128, M), F32),
            pltpu.VMEM((NK, 128, M), F32),
            pltpu.VMEM((NK, 128, M), F32),
            pltpu.VMEM((NK, 4, 4, ROWS, M), BF16),
            pltpu.VMEM((4, 4, 4, ROWS, D), F32),
            pltpu.VMEM((NK, 4, 4, ROWS, D), BF16),
            pltpu.VMEM((NK, 2, 2, 2, ROWS, HALF), BF16),
            pltpu.VMEM((NK, 2, 2, 4, ROWS, HALF), BF16),
            pltpu.VMEM((NK, 2, 4, ROWS, HALF), BF16),
            pltpu.VMEM((NK, 2, 3, ROWS, HALF), BF16),
            pltpu.VMEM((NK, ROWS, D), BF16),
            pltpu.VMEM((NK, ROWS, D), BF16),
            pltpu.VMEM((ROWS, D), F32),
            dma((3,)),
            dma((NK, 2, 16)),
            dma((NK, 2, 16)),
            dma((NK,)),
            dma((NK,)),
            dma((NK, 3)),
            dma((NK, 3)),
            dma((NK, 2, 10)),
            dma((NK, 2, 10)),
        ],
        compiler_params=pltpu.CompilerParams(
            collective_id=1, has_side_effects=True, vmem_limit_bytes=61 * 1024 * 1024
        ),
        cost_estimate=pl.CostEstimate(flops=8 * 1024 * D * M, bytes_accessed=9 * 1024 * 1024, transcendentals=0),
        name="crosscoder",
    )(streams, enc_weight, enc_bias.reshape(1, M), dec_weight)
    return (rows + dec_bias)[None]


def solution(mesh):
    in_specs = (
        P("layer", "latent", None),
        P("layer", None, "latent"),
        P("latent"),
        P("layer", "latent", None),
        P("layer", None),
    )
    return jax.shard_map(
        shards, mesh=mesh, in_specs=in_specs, out_specs=P("layer", "latent", None), check_vma=False
    )
```
